256 devices in a mesh: section: 4 (over x), coil: 32 (over y, z), cuts: 2 (over core).
Axes of the slice: x: 4, y: 4, z: 8, core: 2. Of those that a mesh axis runs over, the one named last changes fastest.
Arguments:
- initial: bfloat16 [2, 32, 80, 2, 128], P(None, 'coil', 'cuts'), may hold values from -6 to 6
- sens: bfloat16 [2, 64, 32, 80, 2, 128], P(None, ('coil', 'cuts')), may hold values from -3.5 to 3.5
- kspace: bfloat16 [2, 64, 32, 80, 2, 128], P(None, ('coil', 'cuts')), may hold values from -6 to 6
- mask: int32 [2, 80, 128], replicated, may hold values 0 or 1
- step_sizes: float32 [4], P('section'), may hold values from 0.3 to 1.5
- conv_in: bfloat16 [4, 128, 18], P('section'), may hold values from -1.5 to 1.5
- bias_in: float32 [4, 128], P('section'), may hold values from -3 to 3
- conv_out: bfloat16 [4, 18, 128], P('section'), may hold values from -0.1875 to 0.1875
Outputs:
- cascade_images: bfloat16 [4, 2, 32, 80, 2, 128], P('section', None, 'coil', 'cuts')
The draws below stay inside these ranges and needn't reach their ends.
Inputs may be any that keep to these rules, and one draw needn't show every extreme that they name: `mask`: 1 marks a sampled phase-encoding line of the slab, 0 one that was not measured.
All inputs are finite; a program needn't handle non-finite values.
Results may differ from the reference program's by a relative error of at most 0.028.
Values may be sent and summed in bfloat16 or wider, within the bound.
A program may use at most 128 MiB of HBM per device.

```python
import math
import jax
import jax.numpy as jnp
from jax import lax

X = 32
Y = 80
Z = 128
HID = 128
SLABS = 2
COILS = 64
CASCADES = 4


def set_ends(drawn, rng, smallest, largest):
    longest = drawn.shape.index(max(drawn.shape))
    spots = []
    for shift in (0, 1):
        where = [jax.random.randint(jax.random.fold_in(rng, axis), (), 0, length) for axis, length in enumerate(drawn.shape)]
        where[longest] = (where[longest] + shift) % drawn.shape[longest]
        spots.append(tuple(where))
    return drawn.at[spots[0]].set(smallest).at[spots[1]].set(largest)


def with_spikes(drawn, rng, source, target, blocks, factor):
    def block_of(axis_at):
        return (jnp.arange(drawn.shape[axis_at]) // (drawn.shape[axis_at] // blocks)).reshape((-1,) + (1,) * (drawn.ndim - 1 - axis_at))

    one_side = jax.random.permutation(rng, blocks)[block_of(target)]
    second = (block_of(target) + blocks // 2) % blocks
    return jnp.where((block_of(source) == one_side) | (block_of(source) == second), factor * drawn, drawn)


def block_levels(stream_key, shape, cuts, smallest, largest):
    factor_of, own = 1.0, jax.random.fold_in(stream_key, 6)
    for dim, parts in cuts:
        heights = jnp.exp(jax.random.uniform(jax.random.fold_in(own, dim), (parts,), jnp.float32, smallest / len(cuts), largest / len(cuts)))
        factor_of = factor_of * jnp.repeat(heights, shape[dim] // parts).reshape([-1 if axis == dim else 1 for axis in range(len(shape))])
    return factor_of


def centred(own_key, extent, scale, bound, cuts=(), held_as=jnp.bfloat16):
    loudness = block_levels(own_key, extent, cuts, -0.22, 0.18) if cuts else 1.0
    drawn = jax.random.normal(own_key, extent, jnp.float32) * scale * loudness
    return jnp.minimum(jnp.maximum(drawn, -bound), bound).astype(held_as)


def heavy_noise(stream_key, extent, scale, bound, pieces, heavy, kind=jnp.bfloat16):
    entries = scale * jax.random.normal(stream_key, extent, jnp.float32)
    if pieces:
        entries = entries * block_levels(stream_key, extent, pieces, -0.22, 0.18)
    return jnp.clip(with_spikes(entries, jax.random.fold_in(stream_key, 3), *heavy), -bound, bound).astype(kind)


def setup_inputs(seed: int = 0) -> dict:
    key_of = jax.random.split(jax.random.key(seed), 9)
    return {
        "initial": centred(key_of[0], (SLABS, X, Y, 2, Z), 1.0, 6.0, ((1, 32), (2, 2))),
        "sens": heavy_noise(key_of[1], (SLABS, COILS, X, Y, 2, Z), 0.12, 3.5, ((1, 64),), (1, 2, 32, 2.75)),
        "kspace": centred(key_of[2], (SLABS, COILS, X, Y, 2, Z), 1.0, 6.0, ((1, 64),)),
        "mask": set_ends((jax.random.randint(key_of[3], (SLABS, Y, Z), 0, 3) < 1).astype(jnp.int32), jax.random.fold_in(key_of[3], 1), 0, 1),
        "step_sizes": jnp.clip(jnp.exp(math.log(1.5) - 1.60943787 * jax.random.uniform(key_of[4], (CASCADES,), jnp.float32) ** block_levels(key_of[4], (CASCADES,), ((0, 4),), -0.2, 0.2)), 0.3, 1.5),
        "conv_in": centred(key_of[5], (CASCADES, HID, 18), 18 ** -0.5, 1.5, ((0, 4),)),
        "bias_in": centred(key_of[6], (CASCADES, HID), 0.5, 3.0, ((0, 4),), jnp.float32),
        "conv_out": centred(key_of[7], (CASCADES, 18, HID), (9 * HID) ** -0.5, 0.1875, ((0, 4),)),
    }


def dft_table(length, sign):
    ramp = jnp.arange(length, dtype=jnp.int32)
    phase = ramp[:, None] * ramp[None, :] % length
    angle = phase.astype(jnp.float32) * (2.0 * math.pi / length)
    scale = 1.0 / math.sqrt(length)
    cosine = jnp.cos(angle) * scale
    sine = jnp.sin(angle) * (scale * sign)
    upper = jnp.concatenate([cosine, -sine], axis=1)
    lower = jnp.concatenate([sine, cosine], axis=1)
    return jnp.concatenate([upper, lower], axis=0).astype(jnp.bfloat16)

def pass_last(volume, table):
    shape = volume.shape
    flat = volume.reshape(-1, shape[-2] * shape[-1])
    return jnp.dot(flat, table, preferred_element_type=jnp.float32).astype(jnp.bfloat16).reshape(shape)

def pass_middle(volume, table):
    length = volume.shape[1]
    split = table.reshape(2, length, 2, length).astype(jnp.float32)
    return jnp.einsum('pjcz,cjdk->pkdz', volume.astype(jnp.float32), split).astype(jnp.bfloat16)

def pass_first(volume, table):
    length = volume.shape[0]
    split = table.reshape(2, length, 2, length).astype(jnp.float32)
    return jnp.einsum('jycz,cjdk->kydz', volume.astype(jnp.float32), split).astype(jnp.bfloat16)

def complex_product(sens, image):
    sens_real = sens[:, :, 0].astype(jnp.float32)
    sens_imag = sens[:, :, 1].astype(jnp.float32)
    image_real = image[:, :, 0].astype(jnp.float32)
    image_imag = image[:, :, 1].astype(jnp.float32)
    return jnp.stack([sens_real * image_real - sens_imag * image_imag, sens_real * image_imag + sens_imag * image_real], axis=2)

def conj_product(sens, back):
    sens_real = sens[:, :, 0].astype(jnp.float32)
    sens_imag = sens[:, :, 1].astype(jnp.float32)
    back_real = back[:, :, 0].astype(jnp.float32)
    back_imag = back[:, :, 1].astype(jnp.float32)
    return jnp.stack([sens_real * back_real + sens_imag * back_imag, sens_real * back_imag - sens_imag * back_real], axis=2)

def refine_block(image, weights_in, bias, weights_out):
    rows = image.shape[1]
    width = image.shape[3]
    padded = jnp.pad(image, ((0, 0), (1, 1), (0, 0), (1, 1)))
    taps = jnp.stack([padded[:, shift_row:shift_row + rows, :, shift_col:shift_col + width] for shift_row in range(3) for shift_col in range(3)], axis=2)
    taps = taps.reshape(image.shape[0], rows, 18, width)
    summed = jnp.einsum('hf,xyfz->xyhz', weights_in.astype(jnp.float32), taps.astype(jnp.float32))
    hidden = jax.nn.silu(summed + bias[None, None, :, None]).astype(jnp.bfloat16)
    product = jnp.einsum('fh,xyhz->xyfz', weights_out.astype(jnp.float32), hidden.astype(jnp.float32))
    beside_all = jnp.pad(product, ((0, 0), (1, 1), (0, 0), (1, 1)))
    total = jnp.zeros(image.shape, jnp.float32)
    for shift_row in range(3):
        for shift_col in range(3):
            first = (3 * shift_row + shift_col) * 2
            total = total + beside_all[:, shift_row:shift_row + rows, first:first + 2, shift_col:shift_col + width]
    return total

def cascade_step(image, sens_slab, kspace_slab, mask_slab, step, weights_in, bias, weights_out):
    size_x, size_y, _, size_z = image.shape
    forward_x, forward_y, forward_z = (dft_table(size_x, 1.0), dft_table(size_y, 1.0), dft_table(size_z, 1.0))
    back_x, back_y, back_z = (dft_table(size_x, -1.0), dft_table(size_y, -1.0), dft_table(size_z, -1.0))
    weight_mask = mask_slab.astype(jnp.float32)[None, :, None, :]

    def one_coil(grad, pair):
        sens_one, data_one = pair
        coil_image = complex_product(sens_one, image).astype(jnp.bfloat16)
        predicted = pass_first(pass_middle(pass_last(coil_image, forward_z), forward_y), forward_x)
        resid = (weight_mask * (data_one.astype(jnp.float32) - predicted.astype(jnp.float32))).astype(jnp.bfloat16)
        back = pass_last(pass_middle(pass_first(resid, back_x), back_y), back_z)
        return (grad + conj_product(sens_one, back), None)
    grad, _ = lax.scan(one_coil, jnp.zeros(image.shape, jnp.float32), (sens_slab, kspace_slab))
    refine = refine_block(image, weights_in, bias, weights_out)
    return (image.astype(jnp.float32) - step * grad + refine).astype(jnp.bfloat16)

def reference(initial, sens, kspace, mask, step_sizes, conv_in, bias_in, conv_out):
    images = [initial[slab] for slab in range(SLABS)]
    stacked = []
    for cascade in range(CASCADES):
        images = [cascade_step(images[slab], sens[slab], kspace[slab], mask[slab], step_sizes[cascade], conv_in[cascade], bias_in[cascade], conv_out[cascade]) for slab in range(SLABS)]
        stacked.append(jnp.stack(images, axis=0))
    return jnp.stack(stacked, axis=0)
```

```python
import functools
import math

import jax
import jax.numpy as jnp
import ml_dtypes
import numpy as np
from jax import lax
from jax.experimental import pallas as pl
from jax.experimental.pallas import tpu as pltpu
from jax.sharding import PartitionSpec as P

MESH = pl.DeviceIdType.MESH
BF = jnp.bfloat16
F32 = jnp.float32
SIZE_X, SIZE_Y, SIZE_Z = 32, 80, 128
ROWS = 2 * SIZE_Y
HID = 128
CASCADES = 4
SLOTS = 16


def dft_table(length, sign):
    ramp = np.arange(length)
    angle = (ramp[:, None] * ramp[None, :] % length) * (2.0 * math.pi / length)
    cosine = np.cos(angle) / math.sqrt(length)
    sine = sign * np.sin(angle) / math.sqrt(length)
    return np.block([[cosine, -sine], [sine, cosine]])


def constants():
    planar = np.arange(ROWS)
    woven = 2 * (planar % SIZE_Y) + planar // SIZE_Y
    deal = np.zeros((ROWS, ROWS))
    deal[planar, woven] = 1.0
    forward_y = dft_table(SIZE_Y, 1.0).T
    back_y = dft_table(SIZE_Y, -1.0).T
    square = np.concatenate([back_y @ deal, forward_y, back_y, deal, deal.T], axis=0)
    wide = np.concatenate([dft_table(SIZE_Z, 1.0), dft_table(SIZE_Z, -1.0)], axis=0)
    taps = np.zeros((SIZE_Y * 8, ROWS + 16))
    gather = np.zeros((ROWS, SIZE_Y * 8))
    for row in range(SIZE_Y):
        taps[row * 8 + 6, ROWS] = 1.0
        for shift in range(3):
            other = row + shift - 1
            if 0 <= other < SIZE_Y:
                for part in range(2):
                    taps[row * 8 + shift * 2 + part, part * SIZE_Y + other] = 1.0
                    gather[part * SIZE_Y + row, other * 8 + shift * 2 + part] = 1.0
    place_in = np.zeros((18, 128))
    place_out = np.zeros((32, 18))
    for shift_row in range(3):
        for shift_col in range(3):
            for part in range(2):
                place = shift_col * 8 + shift_row * 2 + part
                column = (3 * shift_row + shift_col) * 2 + part
                place_in[column, place] = 1.0
                place_out[place, column] = 1.0
    return [part.astype(ml_dtypes.bfloat16) for part in (square, wide, taps, gather, place_in, place_out)]


def twiddles():
    first = np.zeros((2, 4, 4), np.complex128)
    second = np.zeros((2, 4, 4, 4), np.complex128)
    for odd in range(2):
        for k in range(4):
            for a in range(4):
                first[odd, k, a] = np.exp(2j * math.pi * k * (2 * a + odd) / 8)
                for b in range(4):
                    position = 8 * b + 2 * a + odd
                    second[odd, k, b, a] = np.exp(2j * math.pi * k * position / SIZE_X) / math.sqrt(SIZE_X)
    return first, second


def dot(a, b):
    return jnp.dot(a, b, preferred_element_type=F32)


def by_lanes(x):
    return jnp.concatenate([x[:SIZE_Y], x[SIZE_Y:]], axis=1)


def by_rows(x):
    return jnp.concatenate([x[:, :SIZE_Z], x[:, SIZE_Z:]], axis=0)


def swap_pair(x):
    a, b, c, d = x[:SIZE_Y, :SIZE_Z], x[SIZE_Y:, :SIZE_Z], x[:SIZE_Y, SIZE_Z:], x[SIZE_Y:, SIZE_Z:]
    return jnp.concatenate(
        [jnp.concatenate([a, b], axis=1), jnp.concatenate([c, d], axis=1)], axis=0
    )


def swap_back(x):
    a, b, c, d = x[:SIZE_Y, :SIZE_Z], x[:SIZE_Y, SIZE_Z:], x[SIZE_Y:, :SIZE_Z], x[SIZE_Y:, SIZE_Z:]
    return jnp.concatenate(
        [jnp.concatenate([a, b], axis=0), jnp.concatenate([c, d], axis=0)], axis=1
    )


def conj_times(s, t):
    s_real, s_imag = s[:, :SIZE_Z].astype(F32), s[:, SIZE_Z:].astype(F32)
    t_real, t_imag = t[:, :SIZE_Z], t[:, SIZE_Z:]
    return s_real * t_real + s_imag * t_imag, s_real * t_imag - s_imag * t_real


def kernel(
    initial, sens, kspace, mask, step, conv_in, bias, conv_out,
    square_in, wide_in, taps_in, gather_in, place_in, place_out,
    out,
    square, wide, taps_sel, gather_sel,
    kbuf, ubuf, gbuf, tbuf, sown, bpart, brecv, bsum, bin_, btot,
    srecv, splan, ibuf, wbuf, fbuf, mplan, mwoven,
    vbuf, wspec, partial, arrived, tapbuf, prodbuf, obuf,
    local_sem, own_sem, s_send, s_recv, i_send, i_recv, w_send, w_recv,
    x_send, x_recv, b_send, b_recv, r_send, r_recv, o_send, o_recv,
):
    sec, pos, core = lax.axis_index("section"), lax.axis_index("coil"), lax.axis_index("cuts")
    row, col = pos // 8, pos % 8
    odd_col = col % 2
    sign = 1 - 2 * odd_col
    odd = sec % 2
    slab = sec // 2
    home = odd_col == odd

    def at(section, y, z, c):
        return (section, y * 8 + z, c)

    twin = col + sign
    mates = [at(sec, row, col, 1 - core), at(sec, row, twin, core), at(sec, row, twin, 1 - core)]
    others = [((sec + k) % 4, pos, core) for k in (1, 2, 3)]

    def toward(j, dy):
        z = (col + (1 - 2 * (j % 2)) * sign * j + 8) % 8
        y = (row + dy) % 4
        return at(sec, y, z, core), 8 * y + 2 * (z // 2) + odd, y * 4 + z // 2

    loads = [
        pltpu.make_async_copy(square_in, square, local_sem.at[0]),
        pltpu.make_async_copy(kspace.at[slab], kbuf, local_sem.at[1]),
        pltpu.make_async_copy(wide_in, wide, local_sem.at[2]),
        pltpu.make_async_copy(taps_in, taps_sel, local_sem.at[3]),
        pltpu.make_async_copy(gather_in, gather_sel, local_sem.at[4]),
    ]
    own_loads = []
    for slot in range(SLOTS):
        _, position, _ = toward(slot // 4, slot % 4)
        own_loads.append(pltpu.make_async_copy(sens.at[slab, position], sown.at[slot], own_sem.at[slot]))
    for load in loads + own_loads:
        load.start()

    barrier = pltpu.get_barrier_semaphore()
    greet = list(mates) + list(others)
    for offset in (0, 2, -1, -3, -2):
        for dy in range(4):
            if offset or dy:
                greet.append(at(sec, (row + dy) % 4, (col + sign * offset + 8) % 8, core))
    for device in greet:
        pl.semaphore_signal(barrier, inc=1, device_id=device, device_id_type=MESH)
    pl.semaphore_wait(barrier, len(greet))

    def remote(src, dst, send, recv, device):
        return pltpu.make_async_remote_copy(
            src_ref=src, dst_ref=dst, send_sem=send, recv_sem=recv, device_id=device, device_id_type=MESH
        )

    half = pl.multiple_of(core * SIZE_Y, SIZE_Y)
    image_copies = [
        remote(initial.at[slab], ibuf.at[pl.ds(half, SIZE_Y)], i_send.at[k], i_recv.at[core], mates[k])
        for k in range(3)
    ]

    @pl.when(home)
    def _():
        for copy in image_copies:
            copy.start()
        ibuf[pl.ds(half, SIZE_Y)] = initial[slab]

    sens_copies = []
    for slot in range(1, SLOTS):
        device, position, _ = toward(slot // 4, slot % 4)
        sens_copies.append(
            remote(sens.at[slab, position], srecv.at[slot], s_send.at[slot], s_recv.at[slot], device)
        )
    for copy in sens_copies:
        copy.start()

    bias_rows = jnp.broadcast_to(bias[...], (128, 128))
    high = bias_rows.astype(BF).astype(F32)
    middle = (bias_rows - high).astype(BF).astype(F32)
    low = bias_rows - high - middle
    which = lax.broadcasted_iota(jnp.int32, (128, 128), 0)
    stacked = jnp.where(which == 6, high, jnp.where(which == 14, middle, jnp.where(which == 22, low, 0.0)))
    first_layer = dot(conv_in[0], place_in[...]) + stacked.T
    wbuf[sec, 0:128] = (0.5 * first_layer).astype(BF)
    wbuf[sec, 128:160] = dot(place_out[...], conv_out[0]).astype(BF)
    fbuf[sec] = jnp.full((8, 128), step[0], F32)
    net_copies = []
    for k in range(3):
        net_copies.append(remote(wbuf.at[sec], wbuf.at[sec], w_send.at[k], w_recv.at[sec], others[k]))
        net_copies.append(remote(fbuf.at[sec], fbuf.at[sec], w_send.at[3 + k], w_recv.at[4 + sec], others[k]))
    for copy in net_copies:
        copy.start()

    loads[0].wait()
    plane = mask[slab].astype(F32).astype(BF)
    both = jnp.concatenate([plane, plane], axis=0)
    mplan[...] = jnp.concatenate([both, both], axis=1)
    mwoven[...] = dot(square[4 * ROWS : 5 * ROWS], both).astype(BF)
    loads[1].wait()

    fold = (1 - 2 * odd).astype(F32)

    def data_rows(n, _):
        masked = mwoven[...]
        two = jnp.concatenate([kbuf[n] * masked, kbuf[n + 16] * masked], axis=1)
        done = dot(square[0:ROWS], two)
        ubuf[n] = done[:, :SIZE_Z] + fold * done[:, SIZE_Z:]
        return 0

    lax.fori_loop(0, 16, data_rows, 0)

    first, second = twiddles()

    def coefficient(table):
        even_value, odd_value = complex(table[0]), complex(table[1])
        return (
            jnp.where(odd == 0, np.float32(even_value.real), np.float32(odd_value.real)),
            jnp.where(odd == 0, np.float32(even_value.imag), np.float32(odd_value.imag)),
        )

    def weighted(terms):
        real, imag = None, None
        for (w_real, w_imag), (v_real, v_imag) in terms:
            r = w_real * v_real - w_imag * v_imag
            i = w_real * v_imag + w_imag * v_real
            real, imag = (r, i) if real is None else (real + r, imag + i)
        return real, imag

    def x_pass(chunk, _):
        top = pl.multiple_of(chunk * 16, 16)
        below = pl.multiple_of(SIZE_Y + chunk * 16, 16)
        for n in range(4):
            u = [(ubuf[n + 4 * k, pl.ds(top, 16)], ubuf[n + 4 * k, pl.ds(below, 16)]) for k in range(4)]
            for a in range(4):
                real, imag = weighted([(coefficient(first[:, k, a]), u[k]) for k in range(4)])
                gbuf[n * 4 + a, 0:16] = real
                gbuf[n * 4 + a, 16:32] = imag
        for a in range(4):
            g = [(gbuf[n * 4 + a, 0:16], gbuf[n * 4 + a, 16:32]) for n in range(4)]
            for b in range(4):
                real, imag = weighted([(coefficient(second[:, n, b, a]), g[n]) for n in range(4)])
                tbuf[b * 4 + a, pl.ds(top, 16), 0:SIZE_Z] = real.astype(BF)
                tbuf[b * 4 + a, pl.ds(top, 16), SIZE_Z:] = imag.astype(BF)
        return 0

    lax.fori_loop(0, 5, x_pass, 0)
    loads[2].wait()
    for load in own_loads:
        load.wait()

    def share(parity):
        def one(q, _):
            jh = q // 2
            j = 2 * jh + parity
            dy = 2 * (q % 2)
            _, _, e0 = toward(j, dy)
            _, _, e1 = toward(j, dy + 1)
            done = dot(jnp.concatenate([tbuf[e0], tbuf[e1]], axis=0), wide[256:512])
            slot = j * 4 + dy
            pair = dot(square[3 * ROWS : 4 * ROWS], jnp.concatenate([sown[slot], sown[slot + 1]], axis=1))
            pair = swap_pair(pair)
            for k in range(2):
                real, imag = conj_times(pair[k * SIZE_Y : (k + 1) * SIZE_Y], done[k * SIZE_Y : (k + 1) * SIZE_Y])
                bpart[parity, jh * 4 + dy + k] = jnp.concatenate([real, imag], axis=1).astype(BF)
            return 0

        lax.fori_loop(0, 4, one, 0)

    share(1 - core)
    exchange = remote(bpart.at[1 - core], brecv, x_send, x_recv, mates[0])
    exchange.start()
    share(core)
    exchange.wait_recv()

    for q in range(8):
        bsum[q] = (bpart[core, q].astype(F32) + brecv[q].astype(F32)).astype(BF)
    data_copies = []
    for q in range(8):
        device, _, _ = toward(2 * (q // 4) + core, q % 4)
        data_copies.append(remote(bsum.at[q], bin_.at[q], b_send.at[q], b_recv.at[q], device))

    @pl.when(core == 0)
    def _():
        bin_[0] = bsum[0]

    @pl.when(core == 1)
    def _():
        data_copies[0].start()

    for copy in data_copies[1:]:
        copy.start()

    def arrival(index):
        return remote(ibuf.at[pl.ds(index * SIZE_Y, SIZE_Y)], ibuf.at[pl.ds(index * SIZE_Y, SIZE_Y)],
                      i_send.at[0], i_recv.at[index], mates[0])

    @pl.when(jnp.logical_or(jnp.logical_not(home), core == 1))
    def _():
        arrival(0).wait_recv()

    @pl.when(jnp.logical_or(jnp.logical_not(home), core == 0))
    def _():
        arrival(1).wait_recv()

    image = by_lanes(dot(square[3 * ROWS : 4 * ROWS], ibuf[...]))

    for k in range(8):
        if k:
            sens_copies[2 * k - 1].wait_recv()
        sens_copies[2 * k].wait_recv()
        left = sown[0] if k == 0 else srecv[2 * k]
        pair = dot(square[3 * ROWS : 4 * ROWS], jnp.concatenate([left, srecv[2 * k + 1]], axis=1))
        splan[pl.ds(k * ROWS, ROWS)] = swap_pair(pair).astype(BF)

    loads[3].wait()
    loads[4].wait()
    lane = lax.broadcasted_iota(jnp.int32, (ROWS, SIZE_Z), 1)

    def moved_right(x):
        return jnp.where(lane == 0, 0.0, pltpu.roll(x, 1, 1))

    def moved_left(x):
        return jnp.where(lane == SIZE_Z - 1, 0.0, pltpu.roll(x, SIZE_Z - 1, 1))

    def net_arrival(c, buf, index):
        return remote(buf.at[c], buf.at[c], w_send.at[0], w_recv.at[index], others[0])

    for k in range(3):
        other = (sec + k + 1) % 4
        net_arrival(other, wbuf, other).wait_recv()
        net_arrival(other, fbuf, 4 + other).wait_recv()

    def operator(image):
        real, imag = image[:, :SIZE_Z], image[:, SIZE_Z:]
        for k in range(SLOTS):
            s = splan[pl.ds(k * SIZE_Y, SIZE_Y)].astype(F32)
            s_real, s_imag = s[:, :SIZE_Z], s[:, SIZE_Z:]
            v = jnp.concatenate([s_real * real - s_imag * imag, s_real * imag + s_imag * real], axis=1)
            vbuf[pl.ds(k * SIZE_Y, SIZE_Y)] = v.astype(BF)
        for k in range(8):
            spectrum = dot(vbuf[pl.ds(k * ROWS, ROWS)], wide[0:256]).astype(BF)
            wspec[pl.ds(k * ROWS, ROWS)] = swap_back(spectrum)
        for k in range(8):
            predicted = dot(square[ROWS : 2 * ROWS], wspec[pl.ds(k * ROWS, ROWS)]).astype(BF)
            vbuf[pl.ds(k * ROWS, ROWS)] = predicted * mplan[...]
        for k in range(8):
            back = dot(square[2 * ROWS : 3 * ROWS], vbuf[pl.ds(k * ROWS, ROWS)]).astype(BF)
            wspec[pl.ds(k * ROWS, ROWS)] = swap_pair(back)
        total_real, total_imag = jnp.zeros((SIZE_Y, SIZE_Z), F32), jnp.zeros((SIZE_Y, SIZE_Z), F32)
        for k in range(8):
            back = dot(wspec[pl.ds(k * ROWS, ROWS)], wide[256:512])
            for i in range(2):
                s = splan[pl.ds(k * ROWS + i * SIZE_Y, SIZE_Y)]
                r, m = conj_times(s, back[i * SIZE_Y : (i + 1) * SIZE_Y])
                total_real, total_imag = total_real + r, total_imag + m
        return jnp.concatenate([total_real, total_imag], axis=1)

    def refine(image, c):
        planar = by_rows(image)
        three = jnp.concatenate([moved_right(planar), planar, moved_left(planar)], axis=1)
        lift = jnp.where(lax.broadcasted_iota(jnp.int32, (16, 3 * SIZE_Z), 0) == 0, 1.0, 0.0)
        operand = jnp.concatenate([three, lift], axis=0).astype(BF)
        tapbuf[...] = dot(taps_sel[...], operand)
        zero = jnp.zeros((8, SIZE_Z), F32)

        def rows_of(step_index, _):
            for i in range(4):
                base = pl.multiple_of(step_index * 64 + i * 16, 16)
                eight = [tapbuf[pl.ds(base + 8 * k, 8)] for k in range(2)]
                columns = [
                    jnp.concatenate([e[:, 0:128], e[:, 128:256], e[:, 256:384], zero], axis=0) for e in eight
                ]
                near = jnp.concatenate(columns, axis=1).astype(BF)
                pre = dot(wbuf[c, 0:128][:, 0:32], near)
                hidden = (pre + pre * jnp.tanh(pre)).astype(BF)
                product = dot(wbuf[c, 128:160], hidden)
                for k in range(2):
                    for d in range(3):
                        prodbuf[pl.ds(base + 8 * k, 8), d * 128 : (d + 1) * 128] = product[
                            d * 8 : (d + 1) * 8, k * 128 : (k + 1) * 128
                        ]
            return 0

        lax.fori_loop(0, 10, rows_of, 0)
        summed = dot(gather_sel[...], prodbuf[...].astype(BF))
        total = moved_right(summed[:, 0:128]) + summed[:, 128:256] + moved_left(summed[:, 256:384])
        return by_lanes(total)

    def data_arrival(q):
        return remote(bsum.at[q], bin_.at[q], b_send.at[q], b_recv.at[q], mates[0])

    def out_copy(c):
        return remote(obuf.at[c], out.at[slab], o_send.at[c], o_recv.at[slab], (c, pos, core))

    def cascade(c, image):
        sent = operator(image)

        @pl.when(c == 0)
        def _():
            @pl.when(core == 1)
            def _():
                data_arrival(0).wait_recv()

            for q in range(1, 8):
                data_arrival(q).wait_recv()
            total = bin_[0].astype(F32)
            for q in range(1, 8):
                total = total + bin_[q].astype(F32)
            btot[...] = total

        partial[c] = (sent - btot[...]).astype(BF)
        copies = [
            remote(partial.at[c], arrived.at[c, k], r_send.at[c, k], r_recv.at[c, k], mates[k]) for k in range(3)
        ]
        for copy in copies:
            copy.start()
        refined = refine(image, c)
        for copy in copies:
            copy.wait_recv()
        total = partial[c].astype(F32)
        for k in range(3):
            total = total + arrived[c, k].astype(F32)
        updated = (image + fbuf[c, 0:1, 0:1] * total + refined).astype(BF)

        @pl.when(home)
        def _():
            base = pl.multiple_of(4 * ROWS + core * SIZE_Y, 16)
            obuf[c] = dot(square[pl.ds(base, SIZE_Y)], by_rows(updated)).astype(BF)

            @pl.when(c == sec)
            def _():
                out[slab] = obuf[c]

            @pl.when(c != sec)
            def _():
                out_copy(c).start()

        return updated.astype(F32)

    lax.fori_loop(0, CASCADES, cascade, image)

    for c in range(CASCADES):
        for k in range(3):
            remote(partial.at[c], arrived.at[c, k], r_send.at[c, k], r_recv.at[c, k], mates[k]).wait_send()

        @pl.when(jnp.logical_and(home, c != sec))
        def _():
            out_copy(c).wait_send()

    for m in range(2):

        @pl.when(2 * m + odd_col != sec)
        def _():
            remote(obuf.at[0], out.at[m], o_send.at[0], o_recv.at[m], others[0]).wait_recv()

    @pl.when(home)
    def _():
        for copy in image_copies:
            copy.wait_send()

    for copy in sens_copies + net_copies + [exchange] + data_copies[1:]:
        copy.wait_send()

    @pl.when(core == 1)
    def _():
        data_copies[0].wait_send()


def body(initial, sens, kspace, mask, step_sizes, conv_in, bias_in, conv_out):
    slabs = initial.shape[0]
    initial = initial.reshape(slabs, SIZE_Y, SIZE_Z)
    sens = sens.reshape(slabs, SIZE_X, ROWS, SIZE_Z)
    kspace = kspace.reshape(slabs, SIZE_X, ROWS, SIZE_Z)
    tables = [jnp.asarray(part) for part in constants()]
    vmem = pl.BlockSpec(memory_space=pltpu.VMEM)
    hbm = pl.BlockSpec(memory_space=pltpu.HBM)
    smem = pl.BlockSpec(memory_space=pltpu.SMEM)
    dma = pltpu.SemaphoreType.DMA
    slice_shape = (SIZE_Y, 2 * SIZE_Z)
    scratch = [
        pltpu.VMEM((5 * ROWS, ROWS), BF),
        pltpu.VMEM((512, 256), BF),
        pltpu.VMEM((SIZE_Y * 8, ROWS + 16), BF),
        pltpu.VMEM((ROWS, SIZE_Y * 8), BF),
        pltpu.VMEM((SIZE_X, ROWS, SIZE_Z), BF),
        pltpu.VMEM((16, ROWS, SIZE_Z), F32),
        pltpu.VMEM((16, 32, SIZE_Z), F32),
        pltpu.VMEM((16, *slice_shape), BF),
        pltpu.VMEM((SLOTS, ROWS, SIZE_Z), BF),
        pltpu.VMEM((2, 8, *slice_shape), BF),
        pltpu.VMEM((8, *slice_shape), BF),
        pltpu.VMEM((8, *slice_shape), BF),
        pltpu.VMEM((8, *slice_shape), BF),
        pltpu.VMEM(slice_shape, F32),
        pltpu.VMEM((SLOTS, ROWS, SIZE_Z), BF),
        pltpu.VMEM((SLOTS * SIZE_Y, 2 * SIZE_Z), BF),
        pltpu.VMEM((ROWS, SIZE_Z), BF),
        pltpu.VMEM((CASCADES, 160, 128), BF),
        pltpu.VMEM((CASCADES, 8, 128), F32),
        pltpu.VMEM((ROWS, 2 * SIZE_Z), BF),
        pltpu.VMEM((ROWS, SIZE_Z), BF),
        pltpu.VMEM((SLOTS * SIZE_Y, 2 * SIZE_Z), BF),
        pltpu.VMEM((SLOTS * SIZE_Y, 2 * SIZE_Z), BF),
        pltpu.VMEM((CASCADES, *slice_shape), BF),
        pltpu.VMEM((CASCADES, 3, *slice_shape), BF),
        pltpu.VMEM((SIZE_Y * 8, 3 * SIZE_Z), F32),
        pltpu.VMEM((SIZE_Y * 8, 3 * SIZE_Z), F32),
        pltpu.VMEM((CASCADES, SIZE_Y, SIZE_Z), BF),
        dma((5,)),
        dma((SLOTS,)),
        dma((SLOTS,)),
        dma((SLOTS,)),
        dma((3,)),
        dma((2,)),
        dma((6,)),
        dma((8,)),
        dma,
        dma,
        dma((8,)),
        dma((8,)),
        dma((CASCADES, 3)),
        dma((CASCADES, 3)),
        dma((CASCADES,)),
        dma((2,)),
    ]
    result = pl.pallas_call(
        kernel,
        out_shape=jax.ShapeDtypeStruct((slabs, SIZE_Y, SIZE_Z), BF),
        in_specs=[vmem, hbm, hbm, vmem, smem, vmem, vmem, vmem, hbm, hbm, hbm, hbm, vmem, vmem],
        out_specs=vmem,
        scratch_shapes=scratch,
        compiler_params=pltpu.CompilerParams(
            collective_id=0, has_side_effects=True, vmem_limit_bytes=40 << 20
        ),
    )(initial, sens, kspace, mask, step_sizes, conv_in, bias_in, conv_out, *tables)
    return result.reshape(1, slabs, 1, SIZE_Y // 2, 2, SIZE_Z)


def solution(mesh):
    return jax.shard_map(
        body,
        mesh=mesh,
        in_specs=(
            P(None, "coil", "cuts", None, None),
            P(None, ("coil", "cuts"), None, None, None, None),
            P(None, ("coil", "cuts"), None, None, None, None),
            P(),
            P("section"),
            P("section", None, None),
            P("section", None),
            P("section", None, None),
        ),
        out_specs=P("section", None, "coil", "cuts", None, None),
        check_vma=False,
    )
```

```python
import functools
import math

import jax
import jax.numpy as jnp
import ml_dtypes
import numpy as np
from jax import lax
from jax.experimental import pallas as pl
from jax.experimental.pallas import tpu as pltpu
from jax.sharding import PartitionSpec as P

MESH = pl.DeviceIdType.MESH
BF = jnp.bfloat16
F32 = jnp.float32
SIZE_X, SIZE_Y, SIZE_Z = 32, 80, 128
ROWS = 2 * SIZE_Y
HID = 128
CASCADES = 4
SLOTS = 16


def dft_table(length, sign):
    ramp = np.arange(length)
    angle = (ramp[:, None] * ramp[None, :] % length) * (2.0 * math.pi / length)
    cosine = np.cos(angle) / math.sqrt(length)
    sine = sign * np.sin(angle) / math.sqrt(length)
    return np.block([[cosine, -sine], [sine, cosine]])


def constants():
    planar = np.arange(ROWS)
    woven = 2 * (planar % SIZE_Y) + planar // SIZE_Y
    deal = np.zeros((ROWS, ROWS))
    deal[planar, woven] = 1.0
    forward_y = dft_table(SIZE_Y, 1.0).T
    back_y = dft_table(SIZE_Y, -1.0).T
    square = np.concatenate([back_y @ deal, forward_y, back_y, deal, deal.T], axis=0)
    wide = np.concatenate([dft_table(SIZE_Z, 1.0), dft_table(SIZE_Z, -1.0)], axis=0)
    taps = np.zeros((SIZE_Y * 8, ROWS + 16))
    gather = np.zeros((ROWS, SIZE_Y * 8))
    for row in range(SIZE_Y):
        taps[row * 8 + 6, ROWS] = 1.0
        for shift in range(3):
            other = row + shift - 1
            if 0 <= other < SIZE_Y:
                for part in range(2):
                    taps[row * 8 + shift * 2 + part, part * SIZE_Y + other] = 1.0
                    gather[part * SIZE_Y + row, other * 8 + shift * 2 + part] = 1.0
    place = np.zeros((32, ROWS))
    for shift_row in range(3):
        for shift_col in range(3):
            for part in range(2):
                place[shift_col * 8 + shift_row * 2 + part, (3 * shift_row + shift_col) * 2 + part] = 1.0
    spread = np.zeros((32, 8 * 256))
    fold = np.zeros((2 * 48, ROWS))
    for shift_col in range(3):
        for r in range(8):
            for i in range(8):
                spread[shift_col * 8 + r, i * 256 + shift_col * 64 + i * 8 + r] = 1.0
            for i in range(2):
                fold[i * 48 + shift_col * 16 + i * 8 + r, shift_col * 8 + r] = 1.0
    square = np.concatenate([square, place, fold], axis=0)
    return [part.astype(ml_dtypes.bfloat16) for part in (square, wide, taps, gather, spread)]


def twiddles():
    first = np.zeros((2, 4, 4), np.complex128)
    second = np.zeros((2, 4, 4, 4), np.complex128)
    for odd in range(2):
        for k in range(4):
            for a in range(4):
                first[odd, k, a] = np.exp(2j * math.pi * k * (2 * a + odd) / 8)
                for b in range(4):
                    position = 8 * b + 2 * a + odd
                    second[odd, k, b, a] = np.exp(2j * math.pi * k * position / SIZE_X) / math.sqrt(SIZE_X)
    return first, second


def dot(a, b):
    return jnp.dot(a, b, preferred_element_type=F32)


def by_lanes(x):
    return jnp.concatenate([x[:SIZE_Y], x[SIZE_Y:]], axis=1)


def by_rows(x):
    return jnp.concatenate([x[:, :SIZE_Z], x[:, SIZE_Z:]], axis=0)


def swap_pair(x):
    a, b, c, d = x[:SIZE_Y, :SIZE_Z], x[SIZE_Y:, :SIZE_Z], x[:SIZE_Y, SIZE_Z:], x[SIZE_Y:, SIZE_Z:]
    return jnp.concatenate(
        [jnp.concatenate([a, b], axis=1), jnp.concatenate([c, d], axis=1)], axis=0
    )


def swap_back(x):
    a, b, c, d = x[:SIZE_Y, :SIZE_Z], x[:SIZE_Y, SIZE_Z:], x[SIZE_Y:, :SIZE_Z], x[SIZE_Y:, SIZE_Z:]
    return jnp.concatenate(
        [jnp.concatenate([a, b], axis=0), jnp.concatenate([c, d], axis=0)], axis=1
    )


def conj_times(s, t):
    s_real, s_imag = s[:, :SIZE_Z].astype(F32), s[:, SIZE_Z:].astype(F32)
    t_real, t_imag = t[:, :SIZE_Z], t[:, SIZE_Z:]
    return s_real * t_real + s_imag * t_imag, s_real * t_imag - s_imag * t_real


def kernel(
    initial, sens, kspace, mask, step, conv_in, bias, conv_out,
    square_in, wide_in, taps_in, gather_in, spread_in,
    out,
    square, wide, taps_sel, gather_sel, spread, first_block, second_block, mask_here, conv_in_here, bias_here, conv_out_here,
    kbuf, ubuf, gbuf, tbuf, sown, bpart, brecv, bsum, bin_, btot,
    srecv, splan, ibuf, wbuf, fbuf, mplan, mwoven,
    vbuf, wspec, partial, arrived, tapbuf, hidbuf, prodbuf, obuf,
    local_sem, own_sem, s_send, s_recv, i_send, i_recv, w_send, w_recv,
    x_send, x_recv, b_send, b_recv, r_send, r_recv, o_send, o_recv,
):
    sec, pos, core = lax.axis_index("section"), lax.axis_index("coil"), lax.axis_index("cuts")
    row, col = pos // 8, pos % 8
    odd_col = col % 2
    sign = 1 - 2 * odd_col
    odd = sec % 2
    slab = sec // 2
    home = odd_col == odd

    def at(section, y, z, c):
        return (section, y * 8 + z, c)

    twin = col + sign
    mates = [at(sec, row, col, 1 - core), at(sec, row, twin, core), at(sec, row, twin, 1 - core)]
    others = [((sec + k) % 4, pos, core) for k in (1, 2, 3)]

    def toward(j, dy):
        z = (col + (1 - 2 * (j % 2)) * sign * j + 8) % 8
        y = (row + dy) % 4
        return at(sec, y, z, core), 8 * y + 2 * (z // 2) + odd, y * 4 + z // 2

    loads = [
        pltpu.make_async_copy(square_in, square, local_sem.at[0]),
        pltpu.make_async_copy(kspace.at[slab], kbuf, local_sem.at[1]),
        pltpu.make_async_copy(wide_in, wide, local_sem.at[2]),
        pltpu.make_async_copy(taps_in, taps_sel, local_sem.at[3]),
        pltpu.make_async_copy(gather_in, gather_sel, local_sem.at[4]),
        pltpu.make_async_copy(mask.at[slab], mask_here, local_sem.at[5]),
        pltpu.make_async_copy(conv_in, conv_in_here, local_sem.at[6]),
        pltpu.make_async_copy(bias, bias_here, local_sem.at[7]),
        pltpu.make_async_copy(conv_out, conv_out_here, local_sem.at[8]),
        pltpu.make_async_copy(spread_in, spread, local_sem.at[10]),
    ]
    half = pl.multiple_of(core * SIZE_Y, SIZE_Y)
    own_half = pltpu.make_async_copy(initial.at[slab], ibuf.at[pl.ds(half, SIZE_Y)], local_sem.at[9])
    own_loads = []
    for slot in range(SLOTS):
        _, position, _ = toward(slot // 4, slot % 4)
        own_loads.append(pltpu.make_async_copy(sens.at[slab, position], sown.at[slot], own_sem.at[slot]))
    for load in loads + own_loads:
        load.start()

    barrier = pltpu.get_barrier_semaphore()
    greet = list(mates) + list(others)
    for offset in (0, 2, -1, -3, -2):
        for dy in range(4):
            if offset or dy:
                greet.append(at(sec, (row + dy) % 4, (col + sign * offset + 8) % 8, core))
    for device in greet:
        pl.semaphore_signal(barrier, inc=1, device_id=device, device_id_type=MESH)
    pl.semaphore_wait(barrier, len(greet))

    def remote(src, dst, send, recv, device):
        return pltpu.make_async_remote_copy(
            src_ref=src, dst_ref=dst, send_sem=send, recv_sem=recv, device_id=device, device_id_type=MESH
        )

    image_copies = [
        remote(initial.at[slab], ibuf.at[pl.ds(half, SIZE_Y)], i_send.at[k], i_recv.at[core], mates[k])
        for k in range(3)
    ]

    @pl.when(home)
    def _():
        for copy in image_copies:
            copy.start()
        own_half.start()

    sens_copies = []
    for slot in range(1, SLOTS):
        device, position, _ = toward(slot // 4, slot % 4)
        sens_copies.append(
            remote(sens.at[slab, position], srecv.at[slot], s_send.at[slot], s_recv.at[slot], device)
        )
    for copy in sens_copies:
        copy.start()

    for load in (loads[0], loads[6], loads[7], loads[8]):
        load.wait()
    bias_rows = jnp.broadcast_to(bias_here[...], (32, 128))
    high = bias_rows.astype(BF).astype(F32)
    middle = (bias_rows - high).astype(BF).astype(F32)
    low = bias_rows - high - middle
    which = lax.broadcasted_iota(jnp.int32, (32, 128), 0)
    stacked = jnp.where(which == 6, high, jnp.where(which == 14, middle, jnp.where(which == 22, low, 0.0)))
    place = square[5 * ROWS : 5 * ROWS + 32][:, 0:18]
    first_layer = dot(place, conv_in_here[0]) + stacked
    first_layer = jnp.concatenate([0.5 * first_layer, jnp.zeros((96, 128), F32)], axis=0)
    wbuf[sec, 0:128] = first_layer.T.astype(BF)
    wbuf[sec, 128:160] = dot(place, conv_out_here[0]).astype(BF)
    fbuf[sec] = jnp.full((8, 128), step[0], F32)
    net_copies = []
    for k in range(3):
        net_copies.append(remote(wbuf.at[sec], wbuf.at[sec], w_send.at[k], w_recv.at[sec], others[k]))
        net_copies.append(remote(fbuf.at[sec], fbuf.at[sec], w_send.at[3 + k], w_recv.at[4 + sec], others[k]))
    for copy in net_copies:
        copy.start()

    loads[5].wait()
    plane = mask_here[...].astype(F32).astype(BF)
    both = jnp.concatenate([plane, plane], axis=0)
    mplan[...] = jnp.concatenate([both, both], axis=1)
    mwoven[...] = dot(square[4 * ROWS : 5 * ROWS], both).astype(BF)
    loads[1].wait()

    fold = (1 - 2 * odd).astype(F32)

    def data_rows(n, _):
        masked = mwoven[...]
        two = jnp.concatenate([kbuf[n] * masked, kbuf[n + 16] * masked], axis=1)
        done = dot(square[0:ROWS], two)
        ubuf[n] = done[:, :SIZE_Z] + fold * done[:, SIZE_Z:]
        return 0

    lax.fori_loop(0, 16, data_rows, 0)

    first, second = twiddles()

    def coefficient(table):
        even_value, odd_value = complex(table[0]), complex(table[1])
        return (
            jnp.where(odd == 0, np.float32(even_value.real), np.float32(odd_value.real)),
            jnp.where(odd == 0, np.float32(even_value.imag), np.float32(odd_value.imag)),
        )

    def weighted(terms):
        real, imag = None, None
        for (w_real, w_imag), (v_real, v_imag) in terms:
            r = w_real * v_real - w_imag * v_imag
            i = w_real * v_imag + w_imag * v_real
            real, imag = (r, i) if real is None else (real + r, imag + i)
        return real, imag

    def x_pass(chunk, _):
        top = pl.multiple_of(chunk * 16, 16)
        below = pl.multiple_of(SIZE_Y + chunk * 16, 16)
        for n in range(4):
            u = [(ubuf[n + 4 * k, pl.ds(top, 16)], ubuf[n + 4 * k, pl.ds(below, 16)]) for k in range(4)]
            for a in range(4):
                real, imag = weighted([(coefficient(first[:, k, a]), u[k]) for k in range(4)])
                gbuf[n * 4 + a, 0:16] = real
                gbuf[n * 4 + a, 16:32] = imag
        for a in range(4):
            g = [(gbuf[n * 4 + a, 0:16], gbuf[n * 4 + a, 16:32]) for n in range(4)]
            for b in range(4):
                real, imag = weighted([(coefficient(second[:, n, b, a]), g[n]) for n in range(4)])
                tbuf[b * 4 + a, pl.ds(top, 16), 0:SIZE_Z] = real.astype(BF)
                tbuf[b * 4 + a, pl.ds(top, 16), SIZE_Z:] = imag.astype(BF)
        return 0

    lax.fori_loop(0, 5, x_pass, 0)
    loads[2].wait()
    for load in own_loads:
        load.wait()

    def share(parity):
        def one(q, _):
            jh = q // 2
            j = 2 * jh + parity
            dy = 2 * (q % 2)
            _, _, e0 = toward(j, dy)
            _, _, e1 = toward(j, dy + 1)
            done = dot(jnp.concatenate([tbuf[e0], tbuf[e1]], axis=0), wide[256:512])
            slot = j * 4 + dy
            pair = dot(square[3 * ROWS : 4 * ROWS], jnp.concatenate([sown[slot], sown[slot + 1]], axis=1))
            pair = swap_pair(pair)
            for k in range(2):
                real, imag = conj_times(pair[k * SIZE_Y : (k + 1) * SIZE_Y], done[k * SIZE_Y : (k + 1) * SIZE_Y])
                bpart[parity, jh * 4 + dy + k] = jnp.concatenate([real, imag], axis=1).astype(BF)
            return 0

        lax.fori_loop(0, 4, one, 0)

    share(1 - core)
    exchange = remote(bpart.at[1 - core], brecv, x_send, x_recv, mates[0])
    exchange.start()
    share(core)
    exchange.wait_recv()

    for q in range(8):
        bsum[q] = (bpart[core, q].astype(F32) + brecv[q].astype(F32)).astype(BF)
    data_copies = []
    for q in range(8):
        device, _, _ = toward(2 * (q // 4) + core, q % 4)
        data_copies.append(remote(bsum.at[q], bin_.at[q], b_send.at[q], b_recv.at[q], device))

    @pl.when(core == 0)
    def _():
        bin_[0] = bsum[0]

    @pl.when(core == 1)
    def _():
        data_copies[0].start()

    for copy in data_copies[1:]:
        copy.start()

    def arrival(index):
        return remote(ibuf.at[pl.ds(index * SIZE_Y, SIZE_Y)], ibuf.at[pl.ds(index * SIZE_Y, SIZE_Y)],
                      i_send.at[0], i_recv.at[index], mates[0])

    @pl.when(jnp.logical_or(jnp.logical_not(home), core == 1))
    def _():
        arrival(0).wait_recv()

    @pl.when(jnp.logical_or(jnp.logical_not(home), core == 0))
    def _():
        arrival(1).wait_recv()

    @pl.when(home)
    def _():
        own_half.wait()

    image = by_lanes(dot(square[3 * ROWS : 4 * ROWS], ibuf[...]))

    def net_arrival(c, buf, index):
        return remote(buf.at[c], buf.at[c], w_send.at[0], w_recv.at[index], others[0])

    for k in range(3):
        other = (sec + k + 1) % 4
        net_arrival(other, wbuf, other).wait_recv()
        net_arrival(other, fbuf, 4 + other).wait_recv()

    loads[9].wait()

    def blocks(c, _):
        layer = wbuf[c, 0:128][:, 0:32]
        for i in range(8):
            first_block[c, i * 128 : (i + 1) * 128] = dot(layer, spread[:, i * 256 : (i + 1) * 256]).astype(BF)
        for i in range(2):
            rows = square[5 * ROWS + 32 + 48 * i : 5 * ROWS + 80 + 48 * i][:, 0:32]
            second_block[c, :, i * 128 : (i + 1) * 128] = dot(rows, wbuf[c, 128:160]).astype(BF)
        return 0

    lax.fori_loop(0, CASCADES, blocks, 0)

    for k in range(8):
        if k:
            sens_copies[2 * k - 1].wait_recv()
        sens_copies[2 * k].wait_recv()
        left = sown[0] if k == 0 else srecv[2 * k]
        pair = dot(square[3 * ROWS : 4 * ROWS], jnp.concatenate([left, srecv[2 * k + 1]], axis=1))
        splan[pl.ds(k * ROWS, ROWS)] = swap_pair(pair).astype(BF)

    loads[3].wait()
    loads[4].wait()
    lane = lax.broadcasted_iota(jnp.int32, (ROWS, SIZE_Z), 1)

    def moved_right(x):
        return jnp.where(lane == 0, 0.0, pltpu.roll(x, 1, 1))

    def moved_left(x):
        return jnp.where(lane == SIZE_Z - 1, 0.0, pltpu.roll(x, SIZE_Z - 1, 1))

    def operator(image):
        real, imag = image[:, :SIZE_Z], image[:, SIZE_Z:]
        for k in range(SLOTS):
            s = splan[pl.ds(k * SIZE_Y, SIZE_Y)].astype(F32)
            s_real, s_imag = s[:, :SIZE_Z], s[:, SIZE_Z:]
            v = jnp.concatenate([s_real * real - s_imag * imag, s_real * imag + s_imag * real], axis=1)
            vbuf[pl.ds(k * SIZE_Y, SIZE_Y)] = v.astype(BF)
        for k in range(8):
            spectrum = dot(vbuf[pl.ds(k * ROWS, ROWS)], wide[0:256]).astype(BF)
            wspec[pl.ds(k * ROWS, ROWS)] = swap_back(spectrum)
        for k in range(8):
            predicted = dot(square[ROWS : 2 * ROWS], wspec[pl.ds(k * ROWS, ROWS)]).astype(BF)
            vbuf[pl.ds(k * ROWS, ROWS)] = predicted * mplan[...]
        for k in range(8):
            back = dot(square[2 * ROWS : 3 * ROWS], vbuf[pl.ds(k * ROWS, ROWS)]).astype(BF)
            wspec[pl.ds(k * ROWS, ROWS)] = swap_pair(back)
        total_real, total_imag = jnp.zeros((SIZE_Y, SIZE_Z), F32), jnp.zeros((SIZE_Y, SIZE_Z), F32)
        for k in range(8):
            back = dot(wspec[pl.ds(k * ROWS, ROWS)], wide[256:512])
            for i in range(2):
                s = splan[pl.ds(k * ROWS + i * SIZE_Y, SIZE_Y)]
                r, m = conj_times(s, back[i * SIZE_Y : (i + 1) * SIZE_Y])
                total_real, total_imag = total_real + r, total_imag + m
        return jnp.concatenate([total_real, total_imag], axis=1)

    def refine(image, c):
        planar = by_rows(image)
        three = jnp.concatenate([moved_right(planar), planar, moved_left(planar)], axis=1)
        lift = jnp.where(lax.broadcasted_iota(jnp.int32, (16, 3 * SIZE_Z), 0) == 0, 1.0, 0.0)
        operand = jnp.concatenate([three, lift], axis=0).astype(BF)
        tapbuf[...] = dot(taps_sel[...], operand).astype(BF)
        for g in range(5):
            near = [
                jnp.concatenate(
                    [tapbuf[128 * g + 64 * k : 128 * g + 64 * (k + 1), d * 128 : (d + 1) * 128] for d in range(3)], axis=0
                )
                for k in range(2)
            ]
            near = jnp.concatenate(near, axis=1)
            for t in range(4):
                pre = dot(first_block[c, t * 256 : (t + 1) * 256][:, 0:192], near).astype(BF)
                hidbuf[g * 4 + t] = pre + pre * jnp.tanh(pre)
        for g in range(5):
            for t in range(4):
                product = dot(second_block[c], hidbuf[g * 4 + t]).astype(BF)
                for k in range(2):
                    top = 128 * g + 64 * k + 16 * t
                    for d in range(3):
                        prodbuf[top : top + 16, d * 128 : (d + 1) * 128] = product[
                            d * 16 : (d + 1) * 16, k * 128 : (k + 1) * 128
                        ]
        summed = dot(gather_sel[...], prodbuf[...])
        total = moved_right(summed[:, 0:128]) + summed[:, 128:256] + moved_left(summed[:, 256:384])
        return by_lanes(total)

    def data_arrival(q):
        return remote(bsum.at[q], bin_.at[q], b_send.at[q], b_recv.at[q], mates[0])

    def out_copy(c):
        return remote(obuf.at[c], out.at[slab], o_send.at[c], o_recv.at[slab], (c, pos, core))

    def cascade(c, image):
        sent = operator(image)

        @pl.when(c == 0)
        def _():
            @pl.when(core == 1)
            def _():
                data_arrival(0).wait_recv()

            for q in range(1, 8):
                data_arrival(q).wait_recv()
            total = bin_[0].astype(F32)
            for q in range(1, 8):
                total = total + bin_[q].astype(F32)
            btot[...] = total

        partial[c] = (sent - btot[...]).astype(BF)
        copies = [
            remote(partial.at[c], arrived.at[c, k], r_send.at[c, k], r_recv.at[c, k], mates[k]) for k in range(3)
        ]
        for copy in copies:
            copy.start()
        refined = refine(image, c)
        for copy in copies:
            copy.wait_recv()
        total = partial[c].astype(F32)
        for k in range(3):
            total = total + arrived[c, k].astype(F32)
        updated = (image + fbuf[c, 0:1, 0:1] * total + refined).astype(BF)

        @pl.when(home)
        def _():
            base = pl.multiple_of(4 * ROWS + core * SIZE_Y, 16)
            obuf[c] = dot(square[pl.ds(base, SIZE_Y)], by_rows(updated)).astype(BF)

            @pl.when(c == sec)
            def _():
                out[slab] = obuf[c]

            @pl.when(c != sec)
            def _():
                out_copy(c).start()

        return updated.astype(F32)

    lax.fori_loop(0, CASCADES, cascade, image)

    for c in range(CASCADES):
        for k in range(3):
            remote(partial.at[c], arrived.at[c, k], r_send.at[c, k], r_recv.at[c, k], mates[k]).wait_send()

        @pl.when(jnp.logical_and(home, c != sec))
        def _():
            out_copy(c).wait_send()

    for m in range(2):

        @pl.when(2 * m + odd_col != sec)
        def _():
            remote(obuf.at[0], out.at[m], o_send.at[0], o_recv.at[m], others[0]).wait_recv()

    @pl.when(home)
    def _():
        for copy in image_copies:
            copy.wait_send()

    for copy in sens_copies + net_copies + [exchange] + data_copies[1:]:
        copy.wait_send()

    @pl.when(core == 1)
    def _():
        data_copies[0].wait_send()


def body(initial, sens, kspace, mask, step_sizes, conv_in, bias_in, conv_out):
    slabs = initial.shape[0]
    initial = initial.reshape(slabs, SIZE_Y, SIZE_Z)
    sens = sens.reshape(slabs, SIZE_X, ROWS, SIZE_Z)
    kspace = kspace.reshape(slabs, SIZE_X, ROWS, SIZE_Z)
    conv_in = jnp.swapaxes(conv_in, 1, 2)
    tables = [jnp.asarray(part) for part in constants()]
    vmem = pl.BlockSpec(memory_space=pltpu.VMEM)
    hbm = pl.BlockSpec(memory_space=pltpu.HBM)
    smem = pl.BlockSpec(memory_space=pltpu.SMEM)
    dma = pltpu.SemaphoreType.DMA
    slice_shape = (SIZE_Y, 2 * SIZE_Z)
    scratch = [
        pltpu.VMEM((5 * ROWS + 128, ROWS), BF),
        pltpu.VMEM((512, 256), BF),
        pltpu.VMEM((SIZE_Y * 8, ROWS + 16), BF),
        pltpu.VMEM((ROWS, SIZE_Y * 8), BF),
        pltpu.VMEM((32, 8 * 256), BF),
        pltpu.VMEM((CASCADES, 8 * HID, 256), BF),
        pltpu.VMEM((CASCADES, 48, 2 * HID), BF),
        pltpu.VMEM((SIZE_Y, SIZE_Z), jnp.int32),
        pltpu.VMEM((1, 18, HID), BF),
        pltpu.VMEM((1, HID), F32),
        pltpu.VMEM((1, 18, HID), BF),
        pltpu.VMEM((SIZE_X, ROWS, SIZE_Z), BF),
        pltpu.VMEM((16, ROWS, SIZE_Z), F32),
        pltpu.VMEM((16, 32, SIZE_Z), F32),
        pltpu.VMEM((16, *slice_shape), BF),
        pltpu.VMEM((SLOTS, ROWS, SIZE_Z), BF),
        pltpu.VMEM((2, 8, *slice_shape), BF),
        pltpu.VMEM((8, *slice_shape), BF),
        pltpu.VMEM((8, *slice_shape), BF),
        pltpu.VMEM((8, *slice_shape), BF),
        pltpu.VMEM(slice_shape, F32),
        pltpu.VMEM((SLOTS, ROWS, SIZE_Z), BF),
        pltpu.VMEM((SLOTS * SIZE_Y, 2 * SIZE_Z), BF),
        pltpu.VMEM((ROWS, SIZE_Z), BF),
        pltpu.VMEM((CASCADES, 160, 128), BF),
        pltpu.VMEM((CASCADES, 8, 128), F32),
        pltpu.VMEM((ROWS, 2 * SIZE_Z), BF),
        pltpu.VMEM((ROWS, SIZE_Z), BF),
        pltpu.VMEM((SLOTS * SIZE_Y, 2 * SIZE_Z), BF),
        pltpu.VMEM((SLOTS * SIZE_Y, 2 * SIZE_Z), BF),
        pltpu.VMEM((CASCADES, *slice_shape), BF),
        pltpu.VMEM((CASCADES, 3, *slice_shape), BF),
        pltpu.VMEM((SIZE_Y * 8, 3 * SIZE_Z), BF),
        pltpu.VMEM((20, 256, 256), BF),
        pltpu.VMEM((SIZE_Y * 8, 3 * SIZE_Z), BF),
        pltpu.VMEM((CASCADES, SIZE_Y, SIZE_Z), BF),
        dma((11,)),
        dma((SLOTS,)),
        dma((SLOTS,)),
        dma((SLOTS,)),
        dma((3,)),
        dma((2,)),
        dma((6,)),
        dma((8,)),
        dma,
        dma,
        dma((8,)),
        dma((8,)),
        dma((CASCADES, 3)),
        dma((CASCADES, 3)),
        dma((CASCADES,)),
        dma((2,)),
    ]
    result = pl.pallas_call(
        kernel,
        out_shape=jax.ShapeDtypeStruct((slabs, SIZE_Y, SIZE_Z), BF),
        in_specs=[hbm] * 4 + [smem] + [hbm] * 8,
        out_specs=vmem,
        scratch_shapes=scratch,
        compiler_params=pltpu.CompilerParams(
            collective_id=0, has_side_effects=True, vmem_limit_bytes=62 << 20
        ),
    )(initial, sens, kspace, mask, step_sizes, conv_in, bias_in, conv_out, *tables)
    return result.reshape(1, slabs, 1, SIZE_Y // 2, 2, SIZE_Z)


def solution(mesh):
    return jax.shard_map(
        body,
        mesh=mesh,
        in_specs=(
            P(None, "coil", "cuts", None, None),
            P(None, ("coil", "cuts"), None, None, None, None),
            P(None, ("coil", "cuts"), None, None, None, None),
            P(),
            P("section"),
            P("section", None, None),
            P("section", None),
            P("section", None, None),
        ),
        out_specs=P("section", None, "coil", "cuts", None, None),
        check_vma=False,
    )
```

```python
import functools
import math

import jax
import jax.numpy as jnp
import ml_dtypes
import numpy as np
from jax import lax
from jax.experimental import pallas as pl
from jax.experimental.pallas import tpu as pltpu
from jax.sharding import PartitionSpec as P

MESH = pl.DeviceIdType.MESH
BF = jnp.bfloat16
F32 = jnp.float32
SIZE_X, SIZE_Y, SIZE_Z = 32, 80, 128
ROWS = 2 * SIZE_Y
HID = 128
CASCADES = 4
SLOTS = 16


def dft_table(length, sign):
    ramp = np.arange(length)
    angle = (ramp[:, None] * ramp[None, :] % length) * (2.0 * math.pi / length)
    cosine = np.cos(angle) / math.sqrt(length)
    sine = sign * np.sin(angle) / math.sqrt(length)
    return np.block([[cosine, -sine], [sine, cosine]])


def constants():
    planar = np.arange(ROWS)
    woven = 2 * (planar % SIZE_Y) + planar // SIZE_Y
    deal = np.zeros((ROWS, ROWS))
    deal[planar, woven] = 1.0
    forward_y = dft_table(SIZE_Y, 1.0).T
    back_y = dft_table(SIZE_Y, -1.0).T
    square = np.concatenate([back_y @ deal, forward_y, back_y, deal, deal.T], axis=0)
    wide = np.concatenate([dft_table(SIZE_Z, 1.0), dft_table(SIZE_Z, -1.0)], axis=0)
    taps = np.zeros((SIZE_Y * 8, ROWS + 16))
    gather = np.zeros((ROWS, SIZE_Y * 8))
    for row in range(SIZE_Y):
        taps[row * 8 + 6, ROWS] = 1.0
        for shift in range(3):
            other = row + shift - 1
            if 0 <= other < SIZE_Y:
                for part in range(2):
                    taps[row * 8 + shift * 2 + part, part * SIZE_Y + other] = 1.0
                    gather[part * SIZE_Y + row, other * 8 + shift * 2 + part] = 1.0
    place = np.zeros((32, ROWS))
    for shift_row in range(3):
        for shift_col in range(3):
            for part in range(2):
                place[shift_col * 8 + shift_row * 2 + part, (3 * shift_row + shift_col) * 2 + part] = 1.0
    spread = np.zeros((32, 8 * 256))
    fold = np.zeros((2 * 48, ROWS))
    for shift_col in range(3):
        for r in range(8):
            for i in range(8):
                spread[shift_col * 8 + r, i * 256 + shift_col * 64 + i * 8 + r] = 1.0
            for i in range(2):
                fold[i * 48 + shift_col * 16 + i * 8 + r, shift_col * 8 + r] = 1.0
    square = np.concatenate([square, place, fold], axis=0)
    return [part.astype(ml_dtypes.bfloat16) for part in (square, wide, taps, gather, spread)]


def twiddles():
    first = np.zeros((2, 4, 4), np.complex128)
    second = np.zeros((2, 4, 4, 4), np.complex128)
    for odd in range(2):
        for k in range(4):
            for a in range(4):
                first[odd, k, a] = np.exp(2j * math.pi * k * (2 * a + odd) / 8)
                for b in range(4):
                    position = 8 * b + 2 * a + odd
                    second[odd, k, b, a] = np.exp(2j * math.pi * k * position / SIZE_X) / math.sqrt(SIZE_X)
    return first, second


def dot(a, b):
    return jnp.dot(a, b, preferred_element_type=F32)


def by_lanes(x):
    return jnp.concatenate([x[:SIZE_Y], x[SIZE_Y:]], axis=1)


def by_rows(x):
    return jnp.concatenate([x[:, :SIZE_Z], x[:, SIZE_Z:]], axis=0)


def swap_pair(x):
    a, b, c, d = x[:SIZE_Y, :SIZE_Z], x[SIZE_Y:, :SIZE_Z], x[:SIZE_Y, SIZE_Z:], x[SIZE_Y:, SIZE_Z:]
    return jnp.concatenate(
        [jnp.concatenate([a, b], axis=1), jnp.concatenate([c, d], axis=1)], axis=0
    )


def swap_back(x):
    a, b, c, d = x[:SIZE_Y, :SIZE_Z], x[:SIZE_Y, SIZE_Z:], x[SIZE_Y:, :SIZE_Z], x[SIZE_Y:, SIZE_Z:]
    return jnp.concatenate(
        [jnp.concatenate([a, b], axis=0), jnp.concatenate([c, d], axis=0)], axis=1
    )


def conj_times(s, t):
    s_real, s_imag = s[:, :SIZE_Z].astype(F32), s[:, SIZE_Z:].astype(F32)
    t_real, t_imag = t[:, :SIZE_Z], t[:, SIZE_Z:]
    return s_real * t_real + s_imag * t_imag, s_real * t_imag - s_imag * t_real


def kernel(
    initial, sens, kspace, mask, step, conv_in, bias, conv_out,
    square_in, wide_in, taps_in, gather_in, spread_in,
    out,
    square, wide, taps_sel, gather_sel, spread, first_block, second_block, mask_here, conv_in_here, bias_here, conv_out_here,
    kbuf, ubuf, gbuf, tbuf, sown, bpart, brecv, bsum, yrecv, zsum, bin_, btot,
    srecv, splan, ibuf, wbuf, fbuf, mplan, mwoven,
    vbuf, wspec, partial, arrived, tapbuf, hidbuf, prodbuf, obuf,
    local_sem, own_sem, s_send, s_recv, i_send, i_recv, w_send, w_recv,
    x_send, x_recv, y_send, y_recv, b_send, b_recv, r_send, r_recv, o_send, o_recv,
):
    sec, pos, core = lax.axis_index("section"), lax.axis_index("coil"), lax.axis_index("cuts")
    row, col = pos // 8, pos % 8
    odd_col = col % 2
    sign = 1 - 2 * ((col + row) % 2)
    odd = sec % 2
    slab = sec // 2
    home = odd_col == odd

    def at(section, y, z, c):
        return (section, y * 8 + z, c)

    twin = (col + sign + 8) % 8
    mates = [at(sec, row, col, 1 - core), at(sec, row, twin, core), at(sec, row, twin, 1 - core)]
    others = [((sec + k) % 4, pos, core) for k in (1, 2, 3)]

    def toward(j, dy):
        z = (col + (1 - 2 * (j % 2)) * (1 - 2 * (dy % 2)) * sign * j + 8) % 8
        y = (row + dy) % 4
        pair = (z + 1 - 2 * ((z + y) % 2) + 8) % 8
        held = jnp.where(z % 2 == odd, z, pair)
        return at(sec, y, z, core), 8 * y + held, y * 4 + held // 2

    barrier = pltpu.get_barrier_semaphore()
    greet = [at(sec, (row + dy) % 4, (col - sign * j + 8) % 8, core) for j in (3, 2, 1, 0) for dy in (2, 1, 3, 0)][:-1]
    for device in greet + others + mates:
        pl.semaphore_signal(barrier, inc=1, device_id=device, device_id_type=MESH)

    loads = [
        pltpu.make_async_copy(square_in, square, local_sem.at[0]),
        pltpu.make_async_copy(kspace.at[slab], kbuf, local_sem.at[1]),
        pltpu.make_async_copy(wide_in, wide, local_sem.at[2]),
        pltpu.make_async_copy(taps_in, taps_sel, local_sem.at[3]),
        pltpu.make_async_copy(gather_in, gather_sel, local_sem.at[4]),
        pltpu.make_async_copy(mask.at[slab], mask_here, local_sem.at[5]),
        pltpu.make_async_copy(conv_in, conv_in_here, local_sem.at[6]),
        pltpu.make_async_copy(bias, bias_here, local_sem.at[7]),
        pltpu.make_async_copy(conv_out, conv_out_here, local_sem.at[8]),
        pltpu.make_async_copy(spread_in, spread, local_sem.at[10]),
    ]
    half = pl.multiple_of(core * SIZE_Y, SIZE_Y)
    own_half = pltpu.make_async_copy(initial.at[slab], ibuf.at[pl.ds(half, SIZE_Y)], local_sem.at[9])
    own_loads = []
    for slot in range(SLOTS):
        _, position, _ = toward(slot // 4, slot % 4)
        own_loads.append(pltpu.make_async_copy(sens.at[slab, position], sown.at[slot], own_sem.at[slot]))
    for load in loads + own_loads:
        load.start()

    def remote(src, dst, send, recv, device):
        return pltpu.make_async_remote_copy(
            src_ref=src, dst_ref=dst, send_sem=send, recv_sem=recv, device_id=device, device_id_type=MESH
        )

    for load in (loads[0], loads[5]):
        load.wait()
    plane = mask_here[...].astype(F32).astype(BF)
    both = jnp.concatenate([plane, plane], axis=0)
    mplan[...] = jnp.concatenate([both, both], axis=1)
    mwoven[...] = dot(square[4 * ROWS : 5 * ROWS], both).astype(BF)
    loads[1].wait()

    fold = (1 - 2 * odd).astype(F32)

    def data_rows(n, _):
        masked = mwoven[...]
        two = jnp.concatenate([kbuf[n] * masked, kbuf[n + 16] * masked], axis=1)
        done = dot(square[0:ROWS], two)
        ubuf[n] = done[:, :SIZE_Z] + fold * done[:, SIZE_Z:]
        return 0

    lax.fori_loop(0, 16, data_rows, 0, unroll=4)

    pl.semaphore_wait(barrier, len(greet) + 6)

    image_copies = [
        remote(initial.at[slab], ibuf.at[pl.ds(half, SIZE_Y)], i_send.at[k], i_recv.at[core], mates[k])
        for k in range(3)
    ]

    @pl.when(home)
    def _():
        for copy in image_copies:
            copy.start()
        own_half.start()

    sens_copies = []
    for slot in range(1, SLOTS):
        device, position, _ = toward(slot // 4, slot % 4)
        sens_copies.append(
            remote(sens.at[slab, position], srecv.at[slot], s_send.at[slot], s_recv.at[slot], device)
        )
    for copy in sens_copies:
        copy.start()

    first, second = twiddles()

    def coefficient(table):
        even_value, odd_value = complex(table[0]), complex(table[1])
        return (
            jnp.where(odd == 0, np.float32(even_value.real), np.float32(odd_value.real)),
            jnp.where(odd == 0, np.float32(even_value.imag), np.float32(odd_value.imag)),
        )

    def weighted(terms):
        real, imag = None, None
        for (w_real, w_imag), (v_real, v_imag) in terms:
            r = w_real * v_real - w_imag * v_imag
            i = w_real * v_imag + w_imag * v_real
            real, imag = (r, i) if real is None else (real + r, imag + i)
        return real, imag

    def x_pass(chunk, _):
        top = pl.multiple_of(chunk * 16, 16)
        below = pl.multiple_of(SIZE_Y + chunk * 16, 16)
        for n in range(4):
            u = [(ubuf[n + 4 * k, pl.ds(top, 16)], ubuf[n + 4 * k, pl.ds(below, 16)]) for k in range(4)]
            for a in range(4):
                real, imag = weighted([(coefficient(first[:, k, a]), u[k]) for k in range(4)])
                gbuf[n * 4 + a, 0:16] = real
                gbuf[n * 4 + a, 16:32] = imag
        for a in range(4):
            g = [(gbuf[n * 4 + a, 0:16], gbuf[n * 4 + a, 16:32]) for n in range(4)]
            for b in range(4):
                real, imag = weighted([(coefficient(second[:, n, b, a]), g[n]) for n in range(4)])
                tbuf[b * 4 + a, pl.ds(top, 16), 0:SIZE_Z] = real.astype(BF)
                tbuf[b * 4 + a, pl.ds(top, 16), SIZE_Z:] = imag.astype(BF)
        return 0

    lax.fori_loop(0, 5, x_pass, 0)
    loads[2].wait()
    for load in own_loads:
        load.wait()

    def share(parity):
        def one(q, _):
            jh = q // 2
            j = 2 * jh + parity
            dy = 2 * (q % 2)
            _, _, e0 = toward(j, dy)
            _, _, e1 = toward(j, dy + 1)
            done = dot(jnp.concatenate([tbuf[e0], tbuf[e1]], axis=0), wide[256:512])
            slot = j * 4 + dy
            pair = dot(square[3 * ROWS : 4 * ROWS], jnp.concatenate([sown[slot], sown[slot + 1]], axis=1))
            pair = swap_pair(pair)
            for k in range(2):
                real, imag = conj_times(pair[k * SIZE_Y : (k + 1) * SIZE_Y], done[k * SIZE_Y : (k + 1) * SIZE_Y])
                bpart[parity, (dy + k) * 2 + jh] = jnp.concatenate([real, imag], axis=1).astype(BF)
            return 0

        lax.fori_loop(0, 4, one, 0, unroll=4)

    share(1 - core)
    exchange = remote(bpart.at[1 - core], brecv, x_send, x_recv, mates[0])
    exchange.start()
    share(core)
    exchange.wait_recv()

    for q in range(8):
        bsum[q] = (bpart[core, q].astype(F32) + brecv[q].astype(F32)).astype(BF)
    row_copies = [
        remote(bsum.at[pl.ds(2 * dy, 2)], yrecv.at[dy], y_send.at[dy], y_recv.at[dy], at(sec, (row + dy) % 4, col, core))
        for dy in (1, 2, 3)
    ]
    for copy in row_copies:
        copy.start()

    for load in (loads[6], loads[7], loads[8]):
        load.wait()
    bias_rows = jnp.broadcast_to(bias_here[...], (32, 128))
    high = bias_rows.astype(BF).astype(F32)
    middle = (bias_rows - high).astype(BF).astype(F32)
    low = bias_rows - high - middle
    which = lax.broadcasted_iota(jnp.int32, (32, 128), 0)
    stacked = jnp.where(which == 6, high, jnp.where(which == 14, middle, jnp.where(which == 22, low, 0.0)))
    place = square[5 * ROWS : 5 * ROWS + 32][:, 0:18]
    first_layer = dot(place, conv_in_here[0]) + stacked
    first_layer = jnp.concatenate([0.5 * first_layer, jnp.zeros((96, 128), F32)], axis=0)
    wbuf[sec, 0:128] = first_layer.T.astype(BF)
    wbuf[sec, 128:160] = dot(place, conv_out_here[0]).astype(BF)
    fbuf[sec] = jnp.full((8, 128), step[0], F32)
    net_copies = []
    for k in range(3):
        net_copies.append(remote(wbuf.at[sec], wbuf.at[sec], w_send.at[k], w_recv.at[sec], others[k]))
        net_copies.append(remote(fbuf.at[sec], fbuf.at[sec], w_send.at[3 + k], w_recv.at[4 + sec], others[k]))
    for copy in net_copies:
        copy.start()

    def arrival(index):
        return remote(ibuf.at[pl.ds(index * SIZE_Y, SIZE_Y)], ibuf.at[pl.ds(index * SIZE_Y, SIZE_Y)],
                      i_send.at[0], i_recv.at[index], mates[0])

    @pl.when(jnp.logical_or(jnp.logical_not(home), core == 1))
    def _():
        arrival(0).wait_recv()

    @pl.when(jnp.logical_or(jnp.logical_not(home), core == 0))
    def _():
        arrival(1).wait_recv()

    @pl.when(home)
    def _():
        own_half.wait()

    image = by_lanes(dot(square[3 * ROWS : 4 * ROWS], ibuf[...]))

    def net_arrival(c, buf, index):
        return remote(buf.at[c], buf.at[c], w_send.at[0], w_recv.at[index], others[0])

    for k in range(3):
        other = (sec + k + 1) % 4
        net_arrival(other, wbuf, other).wait_recv()
        net_arrival(other, fbuf, 4 + other).wait_recv()

    loads[9].wait()

    def blocks(c, _):
        layer = wbuf[c, 0:128][:, 0:32]
        for i in range(8):
            first_block[c, i * 128 : (i + 1) * 128] = dot(layer, spread[:, i * 256 : (i + 1) * 256]).astype(BF)
        for i in range(2):
            rows = square[5 * ROWS + 32 + 48 * i : 5 * ROWS + 80 + 48 * i][:, 0:32]
            second_block[c, :, i * 128 : (i + 1) * 128] = dot(rows, wbuf[c, 128:160]).astype(BF)
        return 0

    lax.fori_loop(0, CASCADES, blocks, 0)

    for copy in row_copies:
        copy.wait_recv()
    for jh in range(2):
        total = bsum[jh].astype(F32)
        for dy in range(1, 4):
            total = total + yrecv[dy, jh].astype(F32)
        zsum[jh] = total.astype(BF)
    data_copies = [
        remote(zsum.at[jh], bin_.at[jh], b_send.at[jh], b_recv.at[jh], toward(2 * jh + core, 0)[0]) for jh in range(2)
    ]
    data_copies[1].start()

    @pl.when(core == 0)
    def _():
        bin_[0] = zsum[0]

    @pl.when(core == 1)
    def _():
        data_copies[0].start()

    for k in range(8):
        if k:
            sens_copies[2 * k - 1].wait_recv()
        sens_copies[2 * k].wait_recv()
        left = sown[0] if k == 0 else srecv[2 * k]
        pair = dot(square[3 * ROWS : 4 * ROWS], jnp.concatenate([left, srecv[2 * k + 1]], axis=1))
        splan[pl.ds(k * ROWS, ROWS)] = swap_pair(pair).astype(BF)

    loads[3].wait()
    loads[4].wait()
    lane = lax.broadcasted_iota(jnp.int32, (ROWS, SIZE_Z), 1)

    def moved_right(x):
        return jnp.where(lane == 0, 0.0, pltpu.roll(x, 1, 1))

    def moved_left(x):
        return jnp.where(lane == SIZE_Z - 1, 0.0, pltpu.roll(x, SIZE_Z - 1, 1))

    def operator(image):
        real, imag = image[:, :SIZE_Z], image[:, SIZE_Z:]
        for k in range(SLOTS):
            s = splan[pl.ds(k * SIZE_Y, SIZE_Y)].astype(F32)
            s_real, s_imag = s[:, :SIZE_Z], s[:, SIZE_Z:]
            v = jnp.concatenate([s_real * real - s_imag * imag, s_real * imag + s_imag * real], axis=1)
            vbuf[pl.ds(k * SIZE_Y, SIZE_Y)] = v.astype(BF)
        for k in range(8):
            spectrum = dot(vbuf[pl.ds(k * ROWS, ROWS)], wide[0:256]).astype(BF)
            wspec[pl.ds(k * ROWS, ROWS)] = swap_back(spectrum)
        for k in range(8):
            predicted = dot(square[ROWS : 2 * ROWS], wspec[pl.ds(k * ROWS, ROWS)]).astype(BF)
            vbuf[pl.ds(k * ROWS, ROWS)] = predicted * mplan[...]
        for k in range(8):
            back = dot(square[2 * ROWS : 3 * ROWS], vbuf[pl.ds(k * ROWS, ROWS)]).astype(BF)
            wspec[pl.ds(k * ROWS, ROWS)] = swap_pair(back)
        total_real, total_imag = jnp.zeros((SIZE_Y, SIZE_Z), F32), jnp.zeros((SIZE_Y, SIZE_Z), F32)
        for k in range(8):
            back = dot(wspec[pl.ds(k * ROWS, ROWS)], wide[256:512])
            for i in range(2):
                s = splan[pl.ds(k * ROWS + i * SIZE_Y, SIZE_Y)]
                r, m = conj_times(s, back[i * SIZE_Y : (i + 1) * SIZE_Y])
                total_real, total_imag = total_real + r, total_imag + m
        return jnp.concatenate([total_real, total_imag], axis=1)

    def refine(image, c):
        planar = by_rows(image)
        three = jnp.concatenate([moved_right(planar), planar, moved_left(planar)], axis=1)
        lift = jnp.where(lax.broadcasted_iota(jnp.int32, (16, 3 * SIZE_Z), 0) == 0, 1.0, 0.0)
        operand = jnp.concatenate([three, lift], axis=0).astype(BF)
        tapbuf[...] = dot(taps_sel[...], operand).astype(BF)
        for g in range(5):
            near = [
                jnp.concatenate(
                    [tapbuf[128 * g + 64 * k : 128 * g + 64 * (k + 1), d * 128 : (d + 1) * 128] for d in range(3)], axis=0
                )
                for k in range(2)
            ]
            near = jnp.concatenate(near, axis=1)
            for t in range(4):
                pre = dot(first_block[c, t * 256 : (t + 1) * 256][:, 0:192], near).astype(BF)
                hidbuf[g * 4 + t] = pre + pre * jnp.tanh(pre)
        for g in range(5):
            for t in range(4):
                product = dot(second_block[c], hidbuf[g * 4 + t]).astype(BF)
                for k in range(2):
                    top = 128 * g + 64 * k + 16 * t
                    for d in range(3):
                        prodbuf[top : top + 16, d * 128 : (d + 1) * 128] = product[
                            d * 16 : (d + 1) * 16, k * 128 : (k + 1) * 128
                        ]
        summed = dot(gather_sel[...], prodbuf[...])
        total = moved_right(summed[:, 0:128]) + summed[:, 128:256] + moved_left(summed[:, 256:384])
        return by_lanes(total)

    def data_arrival(q):
        return remote(zsum.at[q], bin_.at[q], b_send.at[q], b_recv.at[q], mates[0])

    def out_copy(c):
        return remote(obuf.at[c], out.at[slab], o_send.at[c], o_recv.at[slab], (c, pos, core))

    def cascade(c, image):
        sent = operator(image)

        @pl.when(c == 0)
        def _():
            @pl.when(core == 1)
            def _():
                data_arrival(0).wait_recv()

            data_arrival(1).wait_recv()
            btot[...] = bin_[0].astype(F32) + bin_[1].astype(F32)

        partial[c] = (sent - btot[...]).astype(BF)
        copies = [
            remote(partial.at[c], arrived.at[c, k], r_send.at[c, k], r_recv.at[c, k], mates[k]) for k in range(3)
        ]
        for copy in copies:
            copy.start()
        refined = refine(image, c)
        for copy in copies:
            copy.wait_recv()
        total = partial[c].astype(F32)
        for k in range(3):
            total = total + arrived[c, k].astype(F32)
        updated = (image + fbuf[c, 0:1, 0:1] * total + refined).astype(BF)

        @pl.when(home)
        def _():
            base = pl.multiple_of(4 * ROWS + core * SIZE_Y, 16)
            obuf[c] = dot(square[pl.ds(base, SIZE_Y)], by_rows(updated)).astype(BF)

            @pl.when(c == sec)
            def _():
                out[slab] = obuf[c]

            @pl.when(c != sec)
            def _():
                out_copy(c).start()

        return updated.astype(F32)

    lax.fori_loop(0, CASCADES, cascade, image)

    for c in range(CASCADES):
        for k in range(3):
            remote(partial.at[c], arrived.at[c, k], r_send.at[c, k], r_recv.at[c, k], mates[k]).wait_send()

        @pl.when(jnp.logical_and(home, c != sec))
        def _():
            out_copy(c).wait_send()

    for m in range(2):

        @pl.when(2 * m + odd_col != sec)
        def _():
            remote(obuf.at[0], out.at[m], o_send.at[0], o_recv.at[m], others[0]).wait_recv()

    @pl.when(home)
    def _():
        for copy in image_copies:
            copy.wait_send()

    for copy in sens_copies + net_copies + [exchange, data_copies[1]] + row_copies:
        copy.wait_send()

    @pl.when(core == 1)
    def _():
        data_copies[0].wait_send()


def body(initial, sens, kspace, mask, step_sizes, conv_in, bias_in, conv_out):
    slabs = initial.shape[0]
    initial = initial.reshape(slabs, SIZE_Y, SIZE_Z)
    sens = sens.reshape(slabs, SIZE_X, ROWS, SIZE_Z)
    kspace = kspace.reshape(slabs, SIZE_X, ROWS, SIZE_Z)
    conv_in = jnp.swapaxes(conv_in, 1, 2)
    tables = [jnp.asarray(part) for part in constants()]
    vmem = pl.BlockSpec(memory_space=pltpu.VMEM)
    hbm = pl.BlockSpec(memory_space=pltpu.HBM)
    smem = pl.BlockSpec(memory_space=pltpu.SMEM)
    dma = pltpu.SemaphoreType.DMA
    slice_shape = (SIZE_Y, 2 * SIZE_Z)
    scratch = [
        pltpu.VMEM((5 * ROWS + 128, ROWS), BF),
        pltpu.VMEM((512, 256), BF),
        pltpu.VMEM((SIZE_Y * 8, ROWS + 16), BF),
        pltpu.VMEM((ROWS, SIZE_Y * 8), BF),
        pltpu.VMEM((32, 8 * 256), BF),
        pltpu.VMEM((CASCADES, 8 * HID, 256), BF),
        pltpu.VMEM((CASCADES, 48, 2 * HID), BF),
        pltpu.VMEM((SIZE_Y, SIZE_Z), jnp.int32),
        pltpu.VMEM((1, 18, HID), BF),
        pltpu.VMEM((1, HID), F32),
        pltpu.VMEM((1, 18, HID), BF),
        pltpu.VMEM((SIZE_X, ROWS, SIZE_Z), BF),
        pltpu.VMEM((16, ROWS, SIZE_Z), F32),
        pltpu.VMEM((16, 32, SIZE_Z), F32),
        pltpu.VMEM((16, *slice_shape), BF),
        pltpu.VMEM((SLOTS, ROWS, SIZE_Z), BF),
        pltpu.VMEM((2, 8, *slice_shape), BF),
        pltpu.VMEM((8, *slice_shape), BF),
        pltpu.VMEM((8, *slice_shape), BF),
        pltpu.VMEM((4, 2, *slice_shape), BF),
        pltpu.VMEM((2, *slice_shape), BF),
        pltpu.VMEM((2, *slice_shape), BF),
        pltpu.VMEM(slice_shape, F32),
        pltpu.VMEM((SLOTS, ROWS, SIZE_Z), BF),
        pltpu.VMEM((SLOTS * SIZE_Y, 2 * SIZE_Z), BF),
        pltpu.VMEM((ROWS, SIZE_Z), BF),
        pltpu.VMEM((CASCADES, 160, 128), BF),
        pltpu.VMEM((CASCADES, 8, 128), F32),
        pltpu.VMEM((ROWS, 2 * SIZE_Z), BF),
        pltpu.VMEM((ROWS, SIZE_Z), BF),
        pltpu.VMEM((SLOTS * SIZE_Y, 2 * SIZE_Z), BF),
        pltpu.VMEM((SLOTS * SIZE_Y, 2 * SIZE_Z), BF),
        pltpu.VMEM((CASCADES, *slice_shape), BF),
        pltpu.VMEM((CASCADES, 3, *slice_shape), BF),
        pltpu.VMEM((SIZE_Y * 8, 3 * SIZE_Z), BF),
        pltpu.VMEM((20, 256, 256), BF),
        pltpu.VMEM((SIZE_Y * 8, 3 * SIZE_Z), BF),
        pltpu.VMEM((CASCADES, SIZE_Y, SIZE_Z), BF),
        dma((11,)),
        dma((SLOTS,)),
        dma((SLOTS,)),
        dma((SLOTS,)),
        dma((3,)),
        dma((2,)),
        dma((6,)),
        dma((8,)),
        dma,
        dma,
        dma((4,)),
        dma((4,)),
        dma((2,)),
        dma((2,)),
        dma((CASCADES, 3)),
        dma((CASCADES, 3)),
        dma((CASCADES,)),
        dma((2,)),
    ]
    result = pl.pallas_call(
        kernel,
        out_shape=jax.ShapeDtypeStruct((slabs, SIZE_Y, SIZE_Z), BF),
        in_specs=[hbm] * 4 + [smem] + [hbm] * 8,
        out_specs=vmem,
        scratch_shapes=scratch,
        compiler_params=pltpu.CompilerParams(
            collective_id=0, has_side_effects=True, vmem_limit_bytes=62 << 20
        ),
    )(initial, sens, kspace, mask, step_sizes, conv_in, bias_in, conv_out, *tables)
    return result.reshape(1, slabs, 1, SIZE_Y // 2, 2, SIZE_Z)


def solution(mesh):
    return jax.shard_map(
        body,
        mesh=mesh,
        in_specs=(
            P(None, "coil", "cuts", None, None),
            P(None, ("coil", "cuts"), None, None, None, None),
            P(None, ("coil", "cuts"), None, None, None, None),
            P(),
            P("section"),
            P("section", None, None),
            P("section", None),
            P("section", None, None),
        ),
        out_specs=P("section", None, "coil", "cuts", None, None),
        check_vma=False,
    )
```

```python
import functools
import math

import jax
import jax.numpy as jnp
import ml_dtypes
import numpy as np
from jax import lax
from jax.experimental import pallas as pl
from jax.experimental.pallas import tpu as pltpu
from jax.sharding import PartitionSpec as P

MESH = pl.DeviceIdType.MESH
BF = jnp.bfloat16
F32 = jnp.float32
SIZE_X, SIZE_Y, SIZE_Z = 32, 80, 128
ROWS = 2 * SIZE_Y
HID = 128
CASCADES = 4
SLOTS = 16


def dft_table(length, sign):
    ramp = np.arange(length)
    angle = (ramp[:, None] * ramp[None, :] % length) * (2.0 * math.pi / length)
    cosine = np.cos(angle) / math.sqrt(length)
    sine = sign * np.sin(angle) / math.sqrt(length)
    return np.block([[cosine, -sine], [sine, cosine]])


def constants():
    planar = np.arange(ROWS)
    woven = 2 * (planar % SIZE_Y) + planar // SIZE_Y
    deal = np.zeros((ROWS, ROWS))
    deal[planar, woven] = 1.0
    forward_y = dft_table(SIZE_Y, 1.0).T
    back_y = dft_table(SIZE_Y, -1.0).T
    square = np.concatenate([back_y @ deal, forward_y, back_y, deal, deal.T], axis=0)
    wide = np.concatenate([dft_table(SIZE_Z, 1.0), dft_table(SIZE_Z, -1.0)], axis=0)
    taps = np.zeros((SIZE_Y * 8, ROWS + 16))
    gather = np.zeros((ROWS, SIZE_Y * 8))
    for row in range(SIZE_Y):
        taps[row * 8 + 6, ROWS] = 1.0
        for shift in range(3):
            other = row + shift - 1
            if 0 <= other < SIZE_Y:
                for part in range(2):
                    taps[row * 8 + shift * 2 + part, part * SIZE_Y + other] = 1.0
                    gather[part * SIZE_Y + row, other * 8 + shift * 2 + part] = 1.0
    place = np.zeros((32, ROWS))
    for shift_row in range(3):
        for shift_col in range(3):
            for part in range(2):
                place[shift_col * 8 + shift_row * 2 + part, (3 * shift_row + shift_col) * 2 + part] = 1.0
    spread = np.zeros((32, 8 * 256))
    fold = np.zeros((2 * 48, ROWS))
    for shift_col in range(3):
        for r in range(8):
            for i in range(8):
                spread[shift_col * 8 + r, i * 256 + shift_col * 64 + i * 8 + r] = 1.0
            for i in range(2):
                fold[i * 48 + shift_col * 16 + i * 8 + r, shift_col * 8 + r] = 1.0
    square = np.concatenate([square, place, fold], axis=0)
    return [part.astype(ml_dtypes.bfloat16) for part in (square, wide, taps, gather, spread)]


def twiddles():
    first = np.zeros((2, 4, 4), np.complex128)
    second = np.zeros((2, 4, 4, 4), np.complex128)
    for odd in range(2):
        for k in range(4):
            for a in range(4):
                first[odd, k, a] = np.exp(2j * math.pi * k * (2 * a + odd) / 8)
                for b in range(4):
                    position = 8 * b + 2 * a + odd
                    second[odd, k, b, a] = np.exp(2j * math.pi * k * position / SIZE_X) / math.sqrt(SIZE_X)
    return first, second


def dot(a, b):
    return jnp.dot(a, b, preferred_element_type=F32)


def by_lanes(x):
    return jnp.concatenate([x[:SIZE_Y], x[SIZE_Y:]], axis=1)


def by_rows(x):
    return jnp.concatenate([x[:, :SIZE_Z], x[:, SIZE_Z:]], axis=0)


def swap_pair(x):
    a, b, c, d = x[:SIZE_Y, :SIZE_Z], x[SIZE_Y:, :SIZE_Z], x[:SIZE_Y, SIZE_Z:], x[SIZE_Y:, SIZE_Z:]
    return jnp.concatenate(
        [jnp.concatenate([a, b], axis=1), jnp.concatenate([c, d], axis=1)], axis=0
    )


def swap_back(x):
    a, b, c, d = x[:SIZE_Y, :SIZE_Z], x[:SIZE_Y, SIZE_Z:], x[SIZE_Y:, :SIZE_Z], x[SIZE_Y:, SIZE_Z:]
    return jnp.concatenate(
        [jnp.concatenate([a, b], axis=0), jnp.concatenate([c, d], axis=0)], axis=1
    )


def conj_times(s, t):
    s_real, s_imag = s[:, :SIZE_Z].astype(F32), s[:, SIZE_Z:].astype(F32)
    t_real, t_imag = t[:, :SIZE_Z], t[:, SIZE_Z:]
    return s_real * t_real + s_imag * t_imag, s_real * t_imag - s_imag * t_real


def kernel(
    initial, sens, kspace, mask, step, conv_in, bias, conv_out,
    square_in, wide_in, taps_in, gather_in, spread_in,
    out,
    square, wide, taps_sel, gather_sel, spread, first_block, second_block, mask_here, conv_in_here, bias_here, conv_out_here,
    kbuf, ubuf, gbuf, tbuf, sown, bpart, brecv, bsum, yrecv, zsum, bin_, btot,
    srecv, splan, ibuf, wbuf, fbuf, mplan, mwoven,
    vbuf, wspec, partial, arrived, tapbuf, hidbuf, prodbuf, obuf,
    local_sem, own_sem, s_send, s_recv, i_send, i_recv, w_send, w_recv,
    x_send, x_recv, y_send, y_recv, b_send, b_recv, r_send, r_recv, o_send, o_recv,
):
    sec, pos, core = lax.axis_index("section"), lax.axis_index("coil"), lax.axis_index("cuts")
    row, col = pos // 8, pos % 8
    odd_col = col % 2
    sign = 1 - 2 * ((col + row) % 2)
    odd = sec % 2
    slab = sec // 2
    home = odd_col == odd

    def at(section, y, z, c):
        return (section, y * 8 + z, c)

    twin = (col + sign + 8) % 8
    mates = [at(sec, row, col, 1 - core), at(sec, row, twin, core), at(sec, row, twin, 1 - core)]
    others = [((sec + k) % 4, pos, core) for k in (1, 2, 3)]

    def toward(j, dy):
        z = (col + (1 - 2 * (j % 2)) * (1 - 2 * (dy % 2)) * sign * j + 8) % 8
        y = (row + dy) % 4
        pair = (z + 1 - 2 * ((z + y) % 2) + 8) % 8
        held = jnp.where(z % 2 == odd, z, pair)
        return at(sec, y, z, core), 8 * y + held, y * 4 + held // 2

    barrier = pltpu.get_barrier_semaphore()
    greet = [at(sec, (row + dy) % 4, (col - sign * j + 8) % 8, core) for j in (3, 2, 1, 0) for dy in (2, 1, 3, 0)][:-1]
    for device in greet + others + mates:
        pl.semaphore_signal(barrier, inc=1, device_id=device, device_id_type=MESH)

    loads = [
        pltpu.make_async_copy(square_in, square, local_sem.at[0]),
        pltpu.make_async_copy(kspace.at[slab], kbuf, local_sem.at[1]),
        pltpu.make_async_copy(wide_in, wide, local_sem.at[2]),
        pltpu.make_async_copy(taps_in, taps_sel, local_sem.at[3]),
        pltpu.make_async_copy(gather_in, gather_sel, local_sem.at[4]),
        pltpu.make_async_copy(mask.at[slab], mask_here, local_sem.at[5]),
        pltpu.make_async_copy(conv_in, conv_in_here, local_sem.at[6]),
        pltpu.make_async_copy(bias, bias_here, local_sem.at[7]),
        pltpu.make_async_copy(conv_out, conv_out_here, local_sem.at[8]),
        pltpu.make_async_copy(spread_in, spread, local_sem.at[10]),
    ]
    half = pl.multiple_of(core * SIZE_Y, SIZE_Y)
    own_half = pltpu.make_async_copy(initial.at[slab], ibuf.at[pl.ds(half, SIZE_Y)], local_sem.at[9])
    own_loads = []
    for slot in range(SLOTS):
        _, position, _ = toward(slot // 4, slot % 4)
        own_loads.append(pltpu.make_async_copy(sens.at[slab, position], sown.at[slot], own_sem.at[slot]))
    for load in loads + own_loads:
        load.start()

    def remote(src, dst, send, recv, device):
        return pltpu.make_async_remote_copy(
            src_ref=src, dst_ref=dst, send_sem=send, recv_sem=recv, device_id=device, device_id_type=MESH
        )

    for load in (loads[0], loads[5]):
        load.wait()
    plane = mask_here[...].astype(F32).astype(BF)
    both = jnp.concatenate([plane, plane], axis=0)
    mplan[...] = jnp.concatenate([both, both], axis=1)
    mwoven[...] = dot(square[4 * ROWS : 5 * ROWS], both).astype(BF)
    loads[1].wait()

    fold = (1 - 2 * odd).astype(F32)

    def data_rows(n, _):
        masked = mwoven[...]
        two = jnp.concatenate([kbuf[n] * masked, kbuf[n + 16] * masked], axis=1)
        done = dot(square[0:ROWS], two)
        ubuf[n] = done[:, :SIZE_Z] + fold * done[:, SIZE_Z:]
        return 0

    lax.fori_loop(0, 16, data_rows, 0, unroll=4)

    pl.semaphore_wait(barrier, len(greet) + 6)

    image_copies = [
        remote(initial.at[slab], ibuf.at[pl.ds(half, SIZE_Y)], i_send.at[k], i_recv.at[core], mates[k])
        for k in range(3)
    ]

    @pl.when(home)
    def _():
        for copy in image_copies:
            copy.start()
        own_half.start()

    sens_copies = []
    for slot in range(1, SLOTS):
        device, position, _ = toward(slot // 4, slot % 4)
        sens_copies.append(
            remote(sens.at[slab, position], srecv.at[slot], s_send.at[slot], s_recv.at[slot], device)
        )
    for copy in sens_copies:
        copy.start()

    first, second = twiddles()

    def coefficient(table):
        even_value, odd_value = complex(table[0]), complex(table[1])
        return (
            jnp.where(odd == 0, np.float32(even_value.real), np.float32(odd_value.real)),
            jnp.where(odd == 0, np.float32(even_value.imag), np.float32(odd_value.imag)),
        )

    def weighted(terms):
        real, imag = None, None
        for (w_real, w_imag), (v_real, v_imag) in terms:
            r = w_real * v_real - w_imag * v_imag
            i = w_real * v_imag + w_imag * v_real
            real, imag = (r, i) if real is None else (real + r, imag + i)
        return real, imag

    def x_pass(chunk, _):
        top = pl.multiple_of(chunk * 16, 16)
        below = pl.multiple_of(SIZE_Y + chunk * 16, 16)
        for n in range(4):
            u = [(ubuf[n + 4 * k, pl.ds(top, 16)], ubuf[n + 4 * k, pl.ds(below, 16)]) for k in range(4)]
            for a in range(4):
                real, imag = weighted([(coefficient(first[:, k, a]), u[k]) for k in range(4)])
                gbuf[n * 4 + a, 0:16] = real
                gbuf[n * 4 + a, 16:32] = imag
        for a in range(4):
            g = [(gbuf[n * 4 + a, 0:16], gbuf[n * 4 + a, 16:32]) for n in range(4)]
            for b in range(4):
                real, imag = weighted([(coefficient(second[:, n, b, a]), g[n]) for n in range(4)])
                tbuf[b * 4 + a, pl.ds(top, 16), 0:SIZE_Z] = real.astype(BF)
                tbuf[b * 4 + a, pl.ds(top, 16), SIZE_Z:] = imag.astype(BF)
        return 0

    lax.fori_loop(0, 5, x_pass, 0)
    loads[2].wait()
    for load in own_loads:
        load.wait()

    def share(parity):
        def one(q, _):
            jh = q // 2
            j = 2 * jh + parity
            dy = 2 * (q % 2)
            _, _, e0 = toward(j, dy)
            _, _, e1 = toward(j, dy + 1)
            done = dot(jnp.concatenate([tbuf[e0], tbuf[e1]], axis=0), wide[256:512])
            slot = j * 4 + dy
            pair = dot(square[3 * ROWS : 4 * ROWS], jnp.concatenate([sown[slot], sown[slot + 1]], axis=1))
            pair = swap_pair(pair)
            for k in range(2):
                real, imag = conj_times(pair[k * SIZE_Y : (k + 1) * SIZE_Y], done[k * SIZE_Y : (k + 1) * SIZE_Y])
                bpart[parity, (dy + k) * 2 + jh] = jnp.concatenate([real, imag], axis=1).astype(BF)
            return 0

        lax.fori_loop(0, 4, one, 0, unroll=4)

    share(1 - core)
    exchange = remote(bpart.at[1 - core], brecv, x_send, x_recv, mates[0])
    exchange.start()
    share(core)
    exchange.wait_recv()

    for q in range(8):
        bsum[q] = (bpart[core, q].astype(F32) + brecv[q].astype(F32)).astype(BF)
    row_copies = [
        remote(bsum.at[pl.ds(2 * dy, 2)], yrecv.at[dy], y_send.at[dy], y_recv.at[dy], at(sec, (row + dy) % 4, col, core))
        for dy in (1, 2, 3)
    ]
    for copy in row_copies:
        copy.start()

    for load in (loads[6], loads[7], loads[8]):
        load.wait()
    bias_rows = jnp.broadcast_to(bias_here[...], (32, 128))
    high = bias_rows.astype(BF).astype(F32)
    middle = (bias_rows - high).astype(BF).astype(F32)
    low = bias_rows - high - middle
    which = lax.broadcasted_iota(jnp.int32, (32, 128), 0)
    stacked = jnp.where(which == 6, high, jnp.where(which == 14, middle, jnp.where(which == 22, low, 0.0)))
    place = square[5 * ROWS : 5 * ROWS + 32][:, 0:18]
    first_layer = dot(place, conv_in_here[0]) + stacked
    first_layer = jnp.concatenate([0.5 * first_layer, jnp.zeros((96, 128), F32)], axis=0)
    wbuf[sec, 0:128] = first_layer.T.astype(BF)
    wbuf[sec, 128:160] = dot(place, conv_out_here[0]).astype(BF)
    fbuf[sec] = jnp.full((8, 128), step[0], F32)
    net_copies = []
    for k in range(3):
        net_copies.append(remote(wbuf.at[sec], wbuf.at[sec], w_send.at[k], w_recv.at[sec], others[k]))
        net_copies.append(remote(fbuf.at[sec], fbuf.at[sec], w_send.at[3 + k], w_recv.at[4 + sec], others[k]))
    for copy in net_copies:
        copy.start()

    def arrival(index):
        return remote(ibuf.at[pl.ds(index * SIZE_Y, SIZE_Y)], ibuf.at[pl.ds(index * SIZE_Y, SIZE_Y)],
                      i_send.at[0], i_recv.at[index], mates[0])

    @pl.when(jnp.logical_or(jnp.logical_not(home), core == 1))
    def _():
        arrival(0).wait_recv()

    @pl.when(jnp.logical_or(jnp.logical_not(home), core == 0))
    def _():
        arrival(1).wait_recv()

    @pl.when(home)
    def _():
        own_half.wait()

    image = by_lanes(dot(square[3 * ROWS : 4 * ROWS], ibuf[...]))

    def net_arrival(c, buf, index):
        return remote(buf.at[c], buf.at[c], w_send.at[0], w_recv.at[index], others[0])

    for k in range(3):
        other = (sec + k + 1) % 4
        net_arrival(other, wbuf, other).wait_recv()
        net_arrival(other, fbuf, 4 + other).wait_recv()

    loads[9].wait()

    def blocks(c, _):
        layer = wbuf[c, 0:128][:, 0:32]
        for i in range(8):
            first_block[c, i * 128 : (i + 1) * 128] = dot(layer, spread[:, i * 256 : (i + 1) * 256]).astype(BF)
        for i in range(2):
            rows = square[5 * ROWS + 32 + 48 * i : 5 * ROWS + 80 + 48 * i][:, 0:32]
            second_block[c, :, i * 128 : (i + 1) * 128] = dot(rows, wbuf[c, 128:160]).astype(BF)
        return 0

    lax.fori_loop(0, CASCADES, blocks, 0)

    for copy in row_copies:
        copy.wait_recv()
    for jh in range(2):
        total = bsum[jh].astype(F32)
        for dy in range(1, 4):
            total = total + yrecv[dy, jh].astype(F32)
        zsum[jh] = total.astype(BF)
    data_copies = [
        remote(zsum.at[jh], bin_.at[jh], b_send.at[jh], b_recv.at[jh], toward(2 * jh + core, 0)[0]) for jh in range(2)
    ]
    data_copies[1].start()

    @pl.when(core == 0)
    def _():
        bin_[0] = zsum[0]

    @pl.when(core == 1)
    def _():
        data_copies[0].start()

    for k in range(8):
        if k:
            sens_copies[2 * k - 1].wait_recv()
        sens_copies[2 * k].wait_recv()
        left = sown[0] if k == 0 else srecv[2 * k]
        pair = dot(square[3 * ROWS : 4 * ROWS], jnp.concatenate([left, srecv[2 * k + 1]], axis=1))
        splan[pl.ds(k * ROWS, ROWS)] = swap_pair(pair).astype(BF)

    loads[3].wait()
    loads[4].wait()
    lane = lax.broadcasted_iota(jnp.int32, (ROWS, SIZE_Z), 1)

    def moved_right(x):
        return jnp.where(lane == 0, 0.0, pltpu.roll(x, 1, 1))

    def moved_left(x):
        return jnp.where(lane == SIZE_Z - 1, 0.0, pltpu.roll(x, SIZE_Z - 1, 1))

    def operator(image):
        real, imag = image[:, :SIZE_Z], image[:, SIZE_Z:]
        for k in range(SLOTS):
            s = splan[pl.ds(k * SIZE_Y, SIZE_Y)].astype(F32)
            s_real, s_imag = s[:, :SIZE_Z], s[:, SIZE_Z:]
            v = jnp.concatenate([s_real * real - s_imag * imag, s_real * imag + s_imag * real], axis=1)
            vbuf[pl.ds(k * SIZE_Y, SIZE_Y)] = v.astype(BF)
        for k in range(8):
            spectrum = dot(vbuf[pl.ds(k * ROWS, ROWS)], wide[0:256]).astype(BF)
            wspec[pl.ds(k * ROWS, ROWS)] = swap_back(spectrum)
        for k in range(8):
            predicted = dot(square[ROWS : 2 * ROWS], wspec[pl.ds(k * ROWS, ROWS)]).astype(BF)
            vbuf[pl.ds(k * ROWS, ROWS)] = predicted * mplan[...]
        for k in range(8):
            back = dot(square[2 * ROWS : 3 * ROWS], vbuf[pl.ds(k * ROWS, ROWS)]).astype(BF)
            wspec[pl.ds(k * ROWS, ROWS)] = swap_pair(back)
        total_real, total_imag = jnp.zeros((SIZE_Y, SIZE_Z), F32), jnp.zeros((SIZE_Y, SIZE_Z), F32)
        for k in range(8):
            back = dot(wspec[pl.ds(k * ROWS, ROWS)], wide[256:512])
            for i in range(2):
                s = splan[pl.ds(k * ROWS + i * SIZE_Y, SIZE_Y)]
                r, m = conj_times(s, back[i * SIZE_Y : (i + 1) * SIZE_Y])
                total_real, total_imag = total_real + r, total_imag + m
        return jnp.concatenate([total_real, total_imag], axis=1)

    def refine(image, c):
        planar = by_rows(image)
        three = jnp.concatenate([moved_right(planar), planar, moved_left(planar)], axis=1)
        lift = jnp.where(lax.broadcasted_iota(jnp.int32, (16, 3 * SIZE_Z), 0) == 0, 1.0, 0.0)
        operand = jnp.concatenate([three, lift], axis=0).astype(BF)
        tapbuf[...] = dot(taps_sel[...], operand).astype(BF)
        for g in range(5):
            near = [
                jnp.concatenate(
                    [tapbuf[128 * g + 64 * k : 128 * g + 64 * (k + 1), d * 128 : (d + 1) * 128] for d in range(3)], axis=0
                )
                for k in range(2)
            ]
            near = jnp.concatenate(near, axis=1)
            for t in range(4):
                pre = dot(first_block[c, t * 256 : (t + 1) * 256][:, 0:192], near).astype(BF)
                hidbuf[g * 4 + t] = pre + pre * jnp.tanh(pre)
        for g in range(5):
            for t in range(4):
                product = dot(second_block[c], hidbuf[g * 4 + t]).astype(BF)
                for k in range(2):
                    top = 128 * g + 64 * k + 16 * t
                    for d in range(3):
                        prodbuf[top : top + 16, d * 128 : (d + 1) * 128] = product[
                            d * 16 : (d + 1) * 16, k * 128 : (k + 1) * 128
                        ]
        summed = dot(gather_sel[...], prodbuf[...])
        total = moved_right(summed[:, 0:128]) + summed[:, 128:256] + moved_left(summed[:, 256:384])
        return by_lanes(total)

    def data_arrival(q):
        return remote(zsum.at[q], bin_.at[q], b_send.at[q], b_recv.at[q], mates[0])

    def out_copy(c):
        return remote(obuf.at[c], out.at[slab], o_send.at[c], o_recv.at[slab], (c, pos, core))

    def cascade(c, image):
        sent = operator(image)

        @pl.when(c == 0)
        def _():
            @pl.when(core == 1)
            def _():
                data_arrival(0).wait_recv()

            data_arrival(1).wait_recv()
            btot[...] = bin_[0].astype(F32) + bin_[1].astype(F32)

        partial[c] = (sent - btot[...]).astype(BF)
        copies = [
            remote(partial.at[c], arrived.at[c, k], r_send.at[c, k], r_recv.at[c, k], mates[k]) for k in range(3)
        ]
        for copy in copies:
            copy.start()
        refined = refine(image, c)
        for copy in copies:
            copy.wait_recv()
        total = partial[c].astype(F32)
        for k in range(3):
            total = total + arrived[c, k].astype(F32)
        updated = (image + fbuf[c, 0:1, 0:1] * total + refined).astype(BF)

        @pl.when(home)
        def _():
            base = pl.multiple_of(4 * ROWS + core * SIZE_Y, 16)
            obuf[c] = dot(square[pl.ds(base, SIZE_Y)], by_rows(updated)).astype(BF)

            @pl.when(c == sec)
            def _():
                out[slab] = obuf[c]

            @pl.when(c != sec)
            def _():
                out_copy(c).start()

        return updated.astype(F32)

    lax.fori_loop(0, CASCADES, cascade, image)

    for c in range(CASCADES):
        for k in range(3):
            remote(partial.at[c], arrived.at[c, k], r_send.at[c, k], r_recv.at[c, k], mates[k]).wait_send()

        @pl.when(jnp.logical_and(home, c != sec))
        def _():
            out_copy(c).wait_send()

    for m in range(2):

        @pl.when(2 * m + odd_col != sec)
        def _():
            remote(obuf.at[0], out.at[m], o_send.at[0], o_recv.at[m], others[0]).wait_recv()

    @pl.when(home)
    def _():
        for copy in image_copies:
            copy.wait_send()

    for copy in sens_copies + net_copies + [exchange, data_copies[1]] + row_copies:
        copy.wait_send()

    @pl.when(core == 1)
    def _():
        data_copies[0].wait_send()


def body(initial, sens, kspace, mask, step_sizes, conv_in, bias_in, conv_out):
    slabs = initial.shape[0]
    initial = initial.reshape(slabs, SIZE_Y, SIZE_Z)
    sens = sens.reshape(slabs, SIZE_X, ROWS, SIZE_Z)
    kspace = kspace.reshape(slabs, SIZE_X, ROWS, SIZE_Z)
    conv_in = jnp.swapaxes(conv_in, 1, 2)
    tables = [jnp.asarray(part) for part in constants()]
    vmem = pl.BlockSpec(memory_space=pltpu.VMEM)
    hbm = pl.BlockSpec(memory_space=pltpu.HBM)
    smem = pl.BlockSpec(memory_space=pltpu.SMEM)
    dma = pltpu.SemaphoreType.DMA
    slice_shape = (SIZE_Y, 2 * SIZE_Z)
    scratch = [
        pltpu.VMEM((5 * ROWS + 128, ROWS), BF),
        pltpu.VMEM((512, 256), BF),
        pltpu.VMEM((SIZE_Y * 8, ROWS + 16), BF),
        pltpu.VMEM((ROWS, SIZE_Y * 8), BF),
        pltpu.VMEM((32, 8 * 256), BF),
        pltpu.VMEM((CASCADES, 8 * HID, 256), BF),
        pltpu.VMEM((CASCADES, 48, 2 * HID), BF),
        pltpu.VMEM((SIZE_Y, SIZE_Z), jnp.int32),
        pltpu.VMEM((1, 18, HID), BF),
        pltpu.VMEM((1, HID), F32),
        pltpu.VMEM((1, 18, HID), BF),
        pltpu.VMEM((SIZE_X, ROWS, SIZE_Z), BF),
        pltpu.VMEM((16, ROWS, SIZE_Z), F32),
        pltpu.VMEM((16, 32, SIZE_Z), F32),
        pltpu.VMEM((16, *slice_shape), BF),
        pltpu.VMEM((SLOTS, ROWS, SIZE_Z), BF),
        pltpu.VMEM((2, 8, *slice_shape), BF),
        pltpu.VMEM((8, *slice_shape), BF),
        pltpu.VMEM((8, *slice_shape), BF),
        pltpu.VMEM((4, 2, *slice_shape), BF),
        pltpu.VMEM((2, *slice_shape), BF),
        pltpu.VMEM((2, *slice_shape), BF),
        pltpu.VMEM(slice_shape, F32),
        pltpu.VMEM((SLOTS, ROWS, SIZE_Z), BF),
        pltpu.VMEM((SLOTS * SIZE_Y, 2 * SIZE_Z), BF),
        pltpu.VMEM((ROWS, SIZE_Z), BF),
        pltpu.VMEM((CASCADES, 160, 128), BF),
        pltpu.VMEM((CASCADES, 8, 128), F32),
        pltpu.VMEM((ROWS, 2 * SIZE_Z), BF),
        pltpu.VMEM((ROWS, SIZE_Z), BF),
        pltpu.VMEM((SLOTS * SIZE_Y, 2 * SIZE_Z), BF),
        pltpu.VMEM((SLOTS * SIZE_Y, 2 * SIZE_Z), BF),
        pltpu.VMEM((CASCADES, *slice_shape), BF),
        pltpu.VMEM((CASCADES, 3, *slice_shape), BF),
        pltpu.VMEM((SIZE_Y * 8, 3 * SIZE_Z), BF),
        pltpu.VMEM((20, 256, 256), BF),
        pltpu.VMEM((SIZE_Y * 8, 3 * SIZE_Z), BF),
        pltpu.VMEM((CASCADES, SIZE_Y, SIZE_Z), BF),
        dma((11,)),
        dma((SLOTS,)),
        dma((SLOTS,)),
        dma((SLOTS,)),
        dma((3,)),
        dma((2,)),
        dma((6,)),
        dma((8,)),
        dma,
        dma,
        dma((4,)),
        dma((4,)),
        dma((2,)),
        dma((2,)),
        dma((CASCADES, 3)),
        dma((CASCADES, 3)),
        dma((CASCADES,)),
        dma((2,)),
    ]
    result = pl.pallas_call(
        kernel,
        out_shape=pltpu.VMEM((slabs, SIZE_Y, SIZE_Z), BF),
        in_specs=[hbm] * 4 + [smem] + [hbm] * 8,
        out_specs=vmem,
        scratch_shapes=scratch,
        compiler_params=pltpu.CompilerParams(
            collective_id=0, has_side_effects=True, vmem_limit_bytes=62 << 20
        ),
    )(initial, sens, kspace, mask, step_sizes, conv_in, bias_in, conv_out, *tables)
    return result.reshape(1, slabs, 1, SIZE_Y // 2, 2, SIZE_Z)


def solution(mesh):
    return jax.shard_map(
        body,
        mesh=mesh,
        in_specs=(
            P(None, "coil", "cuts", None, None),
            P(None, ("coil", "cuts"), None, None, None, None),
            P(None, ("coil", "cuts"), None, None, None, None),
            P(),
            P("section"),
            P("section", None, None),
            P("section", None),
            P("section", None, None),
        ),
        out_specs=P("section", None, "coil", "cuts", None, None),
        check_vma=False,
    )
```

```python
import functools
import math

import jax
import jax.numpy as jnp
import ml_dtypes
import numpy as np
from jax import lax
from jax.experimental import pallas as pl
from jax.experimental.pallas import tpu as pltpu
from jax.sharding import PartitionSpec as P

MESH = pl.DeviceIdType.MESH
BF = jnp.bfloat16
F32 = jnp.float32
SIZE_X, SIZE_Y, SIZE_Z = 32, 80, 128
ROWS = 2 * SIZE_Y
HID = 128
CASCADES = 4
SLOTS = 16


def dft_table(length, sign):
    ramp = np.arange(length)
    angle = (ramp[:, None] * ramp[None, :] % length) * (2.0 * math.pi / length)
    cosine = np.cos(angle) / math.sqrt(length)
    sine = sign * np.sin(angle) / math.sqrt(length)
    return np.block([[cosine, -sine], [sine, cosine]])


def constants():
    planar = np.arange(ROWS)
    woven = 2 * (planar % SIZE_Y) + planar // SIZE_Y
    deal = np.zeros((ROWS, ROWS))
    deal[planar, woven] = 1.0
    forward_y = dft_table(SIZE_Y, 1.0).T
    back_y = dft_table(SIZE_Y, -1.0).T
    square = np.concatenate([back_y @ deal, forward_y, back_y, deal, deal.T], axis=0)
    wide = np.concatenate([dft_table(SIZE_Z, 1.0), dft_table(SIZE_Z, -1.0)], axis=0)
    taps = np.zeros((SIZE_Y * 8, ROWS + 16))
    gather = np.zeros((ROWS, SIZE_Y * 8))
    for row in range(SIZE_Y):
        taps[row * 8 + 6, ROWS] = 1.0
        for shift in range(3):
            other = row + shift - 1
            if 0 <= other < SIZE_Y:
                for part in range(2):
                    taps[row * 8 + shift * 2 + part, part * SIZE_Y + other] = 1.0
                    gather[part * SIZE_Y + row, other * 8 + shift * 2 + part] = 1.0
    place = np.zeros((32, ROWS))
    for shift_row in range(3):
        for shift_col in range(3):
            for part in range(2):
                place[shift_col * 8 + shift_row * 2 + part, (3 * shift_row + shift_col) * 2 + part] = 1.0
    spread = np.zeros((32, 8 * 256))
    fold = np.zeros((2 * 48, ROWS))
    for shift_col in range(3):
        for r in range(8):
            for i in range(8):
                spread[shift_col * 8 + r, i * 256 + shift_col * 64 + i * 8 + r] = 1.0
            for i in range(2):
                fold[i * 48 + shift_col * 16 + i * 8 + r, shift_col * 8 + r] = 1.0
    square = np.concatenate([square, place, fold], axis=0)
    return [part.astype(ml_dtypes.bfloat16) for part in (square, wide, taps, gather, spread)]


def twiddles():
    first = np.zeros((2, 4, 4), np.complex128)
    second = np.zeros((2, 4, 4, 4), np.complex128)
    for odd in range(2):
        for k in range(4):
            for a in range(4):
                first[odd, k, a] = np.exp(2j * math.pi * k * (2 * a + odd) / 8)
                for b in range(4):
                    position = 8 * b + 2 * a + odd
                    second[odd, k, b, a] = np.exp(2j * math.pi * k * position / SIZE_X) / math.sqrt(SIZE_X)
    return first, second


def dot(a, b):
    return jnp.dot(a, b, preferred_element_type=F32)


def by_lanes(x):
    return jnp.concatenate([x[:SIZE_Y], x[SIZE_Y:]], axis=1)


def by_rows(x):
    return jnp.concatenate([x[:, :SIZE_Z], x[:, SIZE_Z:]], axis=0)


def swap_pair(x):
    a, b, c, d = x[:SIZE_Y, :SIZE_Z], x[SIZE_Y:, :SIZE_Z], x[:SIZE_Y, SIZE_Z:], x[SIZE_Y:, SIZE_Z:]
    return jnp.concatenate(
        [jnp.concatenate([a, b], axis=1), jnp.concatenate([c, d], axis=1)], axis=0
    )


def swap_back(x):
    a, b, c, d = x[:SIZE_Y, :SIZE_Z], x[:SIZE_Y, SIZE_Z:], x[SIZE_Y:, :SIZE_Z], x[SIZE_Y:, SIZE_Z:]
    return jnp.concatenate(
        [jnp.concatenate([a, b], axis=0), jnp.concatenate([c, d], axis=0)], axis=1
    )


def conj_times(s, t):
    s_real, s_imag = s[:, :SIZE_Z].astype(F32), s[:, SIZE_Z:].astype(F32)
    t_real, t_imag = t[:, :SIZE_Z], t[:, SIZE_Z:]
    return s_real * t_real + s_imag * t_imag, s_real * t_imag - s_imag * t_real


def kernel(
    initial, sens, kspace, mask, step, conv_in, bias, conv_out,
    square_in, wide_in, taps_in, gather_in, spread_in,
    out,
    square, wide, taps_sel, gather_sel, spread, first_block, second_block, mask_here, conv_in_here, bias_here, conv_out_here,
    kbuf, ubuf, gbuf, tbuf, sown, bpart, brecv, bsum, yrecv, zsum, bin_, btot,
    srecv, splan, ibuf, wbuf, fbuf, mplan, mwoven,
    vbuf, wspec, partial, arrived, tapbuf, hidbuf, prodbuf, obuf,
    local_sem, own_sem, s_send, s_recv, i_send, i_recv, w_send, w_recv,
    x_send, x_recv, y_send, y_recv, b_send, b_recv, r_send, r_recv, o_send, o_recv,
):
    sec, pos, core = lax.axis_index("section"), lax.axis_index("coil"), lax.axis_index("cuts")
    row, col = pos // 8, pos % 8
    odd_col = col % 2
    sign = 1 - 2 * ((col + row) % 2)
    odd = sec % 2
    slab = sec // 2
    home = odd_col == odd

    def at(section, y, z, c):
        return (section, y * 8 + z, c)

    twin = (col + sign + 8) % 8
    mates = [at(sec, row, col, 1 - core), at(sec, row, twin, core), at(sec, row, twin, 1 - core)]
    others = [((sec + k) % 4, pos, core) for k in (1, 2, 3)]

    def toward(j, dy):
        z = (col + (1 - 2 * (j % 2)) * (1 - 2 * (dy % 2)) * sign * j + 8) % 8
        y = (row + dy) % 4
        pair = (z + 1 - 2 * ((z + y) % 2) + 8) % 8
        held = jnp.where(z % 2 == odd, z, pair)
        return at(sec, y, z, core), 8 * y + held, y * 4 + held // 2

    barrier = pltpu.get_barrier_semaphore()
    greet = [at(sec, (row + dy) % 4, (col - sign * j + 8) % 8, core) for j in (3, 2, 1, 0) for dy in (2, 1, 3, 0)][:-1]
    for device in greet + others + mates:
        pl.semaphore_signal(barrier, inc=1, device_id=device, device_id_type=MESH)

    loads = [
        pltpu.make_async_copy(square_in, square, local_sem.at[0]),
        pltpu.make_async_copy(kspace.at[slab], kbuf, local_sem.at[1]),
        pltpu.make_async_copy(wide_in, wide, local_sem.at[2]),
        pltpu.make_async_copy(taps_in, taps_sel, local_sem.at[3]),
        pltpu.make_async_copy(gather_in, gather_sel, local_sem.at[4]),
        pltpu.make_async_copy(mask.at[slab], mask_here, local_sem.at[5]),
        pltpu.make_async_copy(conv_in, conv_in_here, local_sem.at[6]),
        pltpu.make_async_copy(bias, bias_here, local_sem.at[7]),
        pltpu.make_async_copy(conv_out, conv_out_here, local_sem.at[8]),
        pltpu.make_async_copy(spread_in, spread, local_sem.at[10]),
    ]
    half = pl.multiple_of(core * SIZE_Y, SIZE_Y)
    own_half = pltpu.make_async_copy(initial.at[slab], ibuf.at[pl.ds(half, SIZE_Y)], local_sem.at[9])
    own_loads = []
    for slot in range(SLOTS):
        _, position, _ = toward(slot // 4, slot % 4)
        own_loads.append(pltpu.make_async_copy(sens.at[slab, position], sown.at[slot], own_sem.at[slot]))
    for load in loads + own_loads:
        load.start()

    def remote(src, dst, send, recv, device):
        return pltpu.make_async_remote_copy(
            src_ref=src, dst_ref=dst, send_sem=send, recv_sem=recv, device_id=device, device_id_type=MESH
        )

    for load in (loads[0], loads[5]):
        load.wait()
    plane = mask_here[...].astype(F32).astype(BF)
    both = jnp.concatenate([plane, plane], axis=0)
    mplan[...] = jnp.concatenate([both, both], axis=1)
    mwoven[...] = dot(square[4 * ROWS : 5 * ROWS], both).astype(BF)
    loads[1].wait()

    fold = (1 - 2 * odd).astype(F32)

    def data_rows(n, _):
        masked = mwoven[...]
        two = jnp.concatenate([kbuf[n] * masked, kbuf[n + 16] * masked], axis=1)
        done = dot(square[0:ROWS], two)
        ubuf[n] = done[:, :SIZE_Z] + fold * done[:, SIZE_Z:]
        return 0

    lax.fori_loop(0, 16, data_rows, 0, unroll=4)

    arrived[CASCADES - 1] = jnp.zeros((3, SIZE_Y, 2 * SIZE_Z), BF)
    pl.semaphore_wait(barrier, len(greet) + 6)

    image_copies = [
        remote(initial.at[slab], ibuf.at[pl.ds(half, SIZE_Y)], i_send.at[k], i_recv.at[core], mates[k])
        for k in range(3)
    ]

    @pl.when(home)
    def _():
        for copy in image_copies:
            copy.start()
        own_half.start()

    sens_copies = []
    for slot in range(1, SLOTS):
        device, position, _ = toward(slot // 4, slot % 4)
        sens_copies.append(
            remote(sens.at[slab, position], srecv.at[slot], s_send.at[slot], s_recv.at[slot], device)
        )
    for copy in sens_copies:
        copy.start()

    first, second = twiddles()

    def coefficient(table):
        even_value, odd_value = complex(table[0]), complex(table[1])
        return (
            jnp.where(odd == 0, np.float32(even_value.real), np.float32(odd_value.real)),
            jnp.where(odd == 0, np.float32(even_value.imag), np.float32(odd_value.imag)),
        )

    def weighted(terms):
        real, imag = None, None
        for (w_real, w_imag), (v_real, v_imag) in terms:
            r = w_real * v_real - w_imag * v_imag
            i = w_real * v_imag + w_imag * v_real
            real, imag = (r, i) if real is None else (real + r, imag + i)
        return real, imag

    def x_pass(chunk, _):
        top = pl.multiple_of(chunk * 16, 16)
        below = pl.multiple_of(SIZE_Y + chunk * 16, 16)
        for n in range(4):
            u = [(ubuf[n + 4 * k, pl.ds(top, 16)], ubuf[n + 4 * k, pl.ds(below, 16)]) for k in range(4)]
            for a in range(4):
                real, imag = weighted([(coefficient(first[:, k, a]), u[k]) for k in range(4)])
                gbuf[n * 4 + a, 0:16] = real
                gbuf[n * 4 + a, 16:32] = imag
        for a in range(4):
            g = [(gbuf[n * 4 + a, 0:16], gbuf[n * 4 + a, 16:32]) for n in range(4)]
            for b in range(4):
                real, imag = weighted([(coefficient(second[:, n, b, a]), g[n]) for n in range(4)])
                tbuf[b * 4 + a, pl.ds(top, 16), 0:SIZE_Z] = real.astype(BF)
                tbuf[b * 4 + a, pl.ds(top, 16), SIZE_Z:] = imag.astype(BF)
        return 0

    lax.fori_loop(0, 5, x_pass, 0)
    loads[2].wait()
    for load in own_loads:
        load.wait()

    def share(parity):
        def one(q, _):
            jh = q // 2
            j = 2 * jh + parity
            dy = 2 * (q % 2)
            _, _, e0 = toward(j, dy)
            _, _, e1 = toward(j, dy + 1)
            done = dot(jnp.concatenate([tbuf[e0], tbuf[e1]], axis=0), wide[256:512])
            slot = j * 4 + dy
            pair = dot(square[3 * ROWS : 4 * ROWS], jnp.concatenate([sown[slot], sown[slot + 1]], axis=1))
            pair = swap_pair(pair)
            for k in range(2):
                real, imag = conj_times(pair[k * SIZE_Y : (k + 1) * SIZE_Y], done[k * SIZE_Y : (k + 1) * SIZE_Y])
                bpart[parity, (dy + k) * 2 + jh] = jnp.concatenate([real, imag], axis=1).astype(BF)
            return 0

        lax.fori_loop(0, 4, one, 0, unroll=4)

    share(1 - core)
    exchange = remote(bpart.at[1 - core], brecv, x_send, x_recv, mates[0])
    exchange.start()
    share(core)
    exchange.wait_recv()

    for q in range(8):
        bsum[q] = (bpart[core, q].astype(F32) + brecv[q].astype(F32)).astype(BF)
    row_copies = [
        remote(bsum.at[pl.ds(2 * dy, 2)], yrecv.at[dy], y_send.at[dy], y_recv.at[dy], at(sec, (row + dy) % 4, col, core))
        for dy in (1, 2, 3)
    ]
    for copy in row_copies:
        copy.start()

    for load in (loads[6], loads[7], loads[8]):
        load.wait()
    bias_rows = jnp.broadcast_to(bias_here[...], (32, 128))
    high = bias_rows.astype(BF).astype(F32)
    middle = (bias_rows - high).astype(BF).astype(F32)
    low = bias_rows - high - middle
    which = lax.broadcasted_iota(jnp.int32, (32, 128), 0)
    stacked = jnp.where(which == 6, high, jnp.where(which == 14, middle, jnp.where(which == 22, low, 0.0)))
    place = square[5 * ROWS : 5 * ROWS + 32][:, 0:18]
    first_layer = dot(place, conv_in_here[0]) + stacked
    first_layer = jnp.concatenate([0.5 * first_layer, jnp.zeros((96, 128), F32)], axis=0)
    wbuf[sec, 0:128] = first_layer.T.astype(BF)
    wbuf[sec, 128:160] = dot(place, conv_out_here[0]).astype(BF)
    fbuf[sec] = jnp.full((8, 128), step[0], F32)
    net_copies = []
    for k in range(3):
        net_copies.append(remote(wbuf.at[sec], wbuf.at[sec], w_send.at[k], w_recv.at[sec], others[k]))
        net_copies.append(remote(fbuf.at[sec], fbuf.at[sec], w_send.at[3 + k], w_recv.at[4 + sec], others[k]))
    for copy in net_copies:
        copy.start()

    def arrival(index):
        return remote(ibuf.at[pl.ds(index * SIZE_Y, SIZE_Y)], ibuf.at[pl.ds(index * SIZE_Y, SIZE_Y)],
                      i_send.at[0], i_recv.at[index], mates[0])

    @pl.when(jnp.logical_or(jnp.logical_not(home), core == 1))
    def _():
        arrival(0).wait_recv()

    @pl.when(jnp.logical_or(jnp.logical_not(home), core == 0))
    def _():
        arrival(1).wait_recv()

    @pl.when(home)
    def _():
        own_half.wait()

    image = by_lanes(dot(square[3 * ROWS : 4 * ROWS], ibuf[...]))

    def net_arrival(c, buf, index):
        return remote(buf.at[c], buf.at[c], w_send.at[0], w_recv.at[index], others[0])

    for k in range(3):
        other = (sec + k + 1) % 4
        net_arrival(other, wbuf, other).wait_recv()
        net_arrival(other, fbuf, 4 + other).wait_recv()

    loads[9].wait()

    def blocks(c, _):
        layer = wbuf[c, 0:128][:, 0:32]
        for i in range(8):
            first_block[c, i * 128 : (i + 1) * 128] = dot(layer, spread[:, i * 256 : (i + 1) * 256]).astype(BF)
        for i in range(2):
            rows = square[5 * ROWS + 32 + 48 * i : 5 * ROWS + 80 + 48 * i][:, 0:32]
            second_block[c, :, i * 128 : (i + 1) * 128] = dot(rows, wbuf[c, 128:160]).astype(BF)
        return 0

    lax.fori_loop(0, CASCADES, blocks, 0)

    for copy in row_copies:
        copy.wait_recv()
    for jh in range(2):
        total = bsum[jh].astype(F32)
        for dy in range(1, 4):
            total = total + yrecv[dy, jh].astype(F32)
        zsum[jh] = total.astype(BF)
    data_copies = [
        remote(zsum.at[jh], bin_.at[jh], b_send.at[jh], b_recv.at[jh], toward(2 * jh + core, 0)[0]) for jh in range(2)
    ]
    data_copies[1].start()

    @pl.when(core == 0)
    def _():
        bin_[0] = zsum[0]

    @pl.when(core == 1)
    def _():
        data_copies[0].start()

    for k in range(8):
        if k:
            sens_copies[2 * k - 1].wait_recv()
        sens_copies[2 * k].wait_recv()
        left = sown[0] if k == 0 else srecv[2 * k]
        pair = dot(square[3 * ROWS : 4 * ROWS], jnp.concatenate([left, srecv[2 * k + 1]], axis=1))
        splan[pl.ds(k * ROWS, ROWS)] = swap_pair(pair).astype(BF)

    loads[3].wait()
    loads[4].wait()
    lane = lax.broadcasted_iota(jnp.int32, (ROWS, SIZE_Z), 1)

    def moved_right(x):
        return jnp.where(lane == 0, 0.0, pltpu.roll(x, 1, 1))

    def moved_left(x):
        return jnp.where(lane == SIZE_Z - 1, 0.0, pltpu.roll(x, SIZE_Z - 1, 1))

    def operator(image):
        real, imag = image[:, :SIZE_Z], image[:, SIZE_Z:]
        for k in range(SLOTS):
            s = splan[pl.ds(k * SIZE_Y, SIZE_Y)].astype(F32)
            s_real, s_imag = s[:, :SIZE_Z], s[:, SIZE_Z:]
            v = jnp.concatenate([s_real * real - s_imag * imag, s_real * imag + s_imag * real], axis=1)
            vbuf[pl.ds(k * SIZE_Y, SIZE_Y)] = v.astype(BF)
        for k in range(8):
            spectrum = dot(vbuf[pl.ds(k * ROWS, ROWS)], wide[0:256]).astype(BF)
            wspec[pl.ds(k * ROWS, ROWS)] = swap_back(spectrum)
        for k in range(8):
            predicted = dot(square[ROWS : 2 * ROWS], wspec[pl.ds(k * ROWS, ROWS)]).astype(BF)
            vbuf[pl.ds(k * ROWS, ROWS)] = predicted * mplan[...]
        for k in range(8):
            back = dot(square[2 * ROWS : 3 * ROWS], vbuf[pl.ds(k * ROWS, ROWS)]).astype(BF)
            wspec[pl.ds(k * ROWS, ROWS)] = swap_pair(back)
        total_real, total_imag = jnp.zeros((SIZE_Y, SIZE_Z), F32), jnp.zeros((SIZE_Y, SIZE_Z), F32)
        for k in range(8):
            back = dot(wspec[pl.ds(k * ROWS, ROWS)], wide[256:512])
            for i in range(2):
                s = splan[pl.ds(k * ROWS + i * SIZE_Y, SIZE_Y)]
                r, m = conj_times(s, back[i * SIZE_Y : (i + 1) * SIZE_Y])
                total_real, total_imag = total_real + r, total_imag + m
        return jnp.concatenate([total_real, total_imag], axis=1)

    def refine(image, c):
        planar = by_rows(image)
        three = jnp.concatenate([moved_right(planar), planar, moved_left(planar)], axis=1)
        lift = jnp.where(lax.broadcasted_iota(jnp.int32, (16, 3 * SIZE_Z), 0) == 0, 1.0, 0.0)
        operand = jnp.concatenate([three, lift], axis=0).astype(BF)
        tapbuf[...] = dot(taps_sel[...], operand).astype(BF)
        for g in range(5):
            near = [
                jnp.concatenate(
                    [tapbuf[128 * g + 64 * k : 128 * g + 64 * (k + 1), d * 128 : (d + 1) * 128] for d in range(3)], axis=0
                )
                for k in range(2)
            ]
            near = jnp.concatenate(near, axis=1)
            for t in range(4):
                pre = dot(first_block[c, t * 256 : (t + 1) * 256][:, 0:192], near).astype(BF)
                hidbuf[g * 4 + t] = pre + pre * jnp.tanh(pre)
        for g in range(5):
            for t in range(4):
                product = dot(second_block[c], hidbuf[g * 4 + t]).astype(BF)
                for k in range(2):
                    top = 128 * g + 64 * k + 16 * t
                    for d in range(3):
                        prodbuf[top : top + 16, d * 128 : (d + 1) * 128] = product[
                            d * 16 : (d + 1) * 16, k * 128 : (k + 1) * 128
                        ]
        summed = dot(gather_sel[...], prodbuf[...])
        total = moved_right(summed[:, 0:128]) + summed[:, 128:256] + moved_left(summed[:, 256:384])
        return by_lanes(total)

    def data_arrival(q):
        return remote(zsum.at[q], bin_.at[q], b_send.at[q], b_recv.at[q], mates[0])

    def out_copy(c):
        return remote(obuf.at[c], out.at[slab], o_send.at[c], o_recv.at[slab], (c, pos, core))

    def last_copy(k, for_core):
        c, rows = CASCADES - 1, pl.ds(pl.multiple_of(32 * for_core, 16), 48)
        return remote(
            partial.at[c, rows], arrived.at[c, k, rows], r_send.at[c, k], r_recv.at[c, k], mates[k]
        )

    last_sends = [last_copy(0, 1 - core), last_copy(1, core), last_copy(2, 1 - core)]

    def cascade(c, image):
        sent = operator(image)

        @pl.when(c == 0)
        def _():
            @pl.when(core == 1)
            def _():
                data_arrival(0).wait_recv()

            data_arrival(1).wait_recv()
            btot[...] = bin_[0].astype(F32) + bin_[1].astype(F32)

        partial[c] = (sent - btot[...]).astype(BF)
        copies = [
            remote(partial.at[c], arrived.at[c, k], r_send.at[c, k], r_recv.at[c, k], mates[k]) for k in range(3)
        ]
        @pl.when(c < CASCADES - 1)
        def _():
            for copy in copies:
                copy.start()

        @pl.when(c == CASCADES - 1)
        def _():
            for copy in last_sends:
                copy.start()

        refined = refine(image, c)

        @pl.when(c < CASCADES - 1)
        def _():
            for copy in copies:
                copy.wait_recv()

        @pl.when(c == CASCADES - 1)
        def _():
            for k in range(3):
                last_copy(k, core).wait_recv()

        total = partial[c].astype(F32)
        for k in range(3):
            total = total + arrived[c, k].astype(F32)
        updated = (image + fbuf[c, 0:1, 0:1] * total + refined).astype(BF)

        @pl.when(home)
        def _():
            base = pl.multiple_of(4 * ROWS + core * SIZE_Y, 16)
            obuf[c] = dot(square[pl.ds(base, SIZE_Y)], by_rows(updated)).astype(BF)

            @pl.when(c == sec)
            def _():
                out[slab] = obuf[c]

            @pl.when(c != sec)
            def _():
                out_copy(c).start()

        return updated.astype(F32)

    lax.fori_loop(0, CASCADES, cascade, image)

    for c in range(CASCADES):
        for k in range(3):
            if c < CASCADES - 1:
                remote(partial.at[c], arrived.at[c, k], r_send.at[c, k], r_recv.at[c, k], mates[k]).wait_send()
            else:
                last_sends[k].wait_send()

        @pl.when(jnp.logical_and(home, c != sec))
        def _():
            out_copy(c).wait_send()

    for m in range(2):

        @pl.when(2 * m + odd_col != sec)
        def _():
            remote(obuf.at[0], out.at[m], o_send.at[0], o_recv.at[m], others[0]).wait_recv()

    @pl.when(home)
    def _():
        for copy in image_copies:
            copy.wait_send()

    for copy in sens_copies + net_copies + [exchange, data_copies[1]] + row_copies:
        copy.wait_send()

    @pl.when(core == 1)
    def _():
        data_copies[0].wait_send()


def body(initial, sens, kspace, mask, step_sizes, conv_in, bias_in, conv_out):
    slabs = initial.shape[0]
    initial = initial.reshape(slabs, SIZE_Y, SIZE_Z)
    sens = sens.reshape(slabs, SIZE_X, ROWS, SIZE_Z)
    kspace = kspace.reshape(slabs, SIZE_X, ROWS, SIZE_Z)
    conv_in = jnp.swapaxes(conv_in, 1, 2)
    tables = [jnp.asarray(part) for part in constants()]
    vmem = pl.BlockSpec(memory_space=pltpu.VMEM)
    hbm = pl.BlockSpec(memory_space=pltpu.HBM)
    smem = pl.BlockSpec(memory_space=pltpu.SMEM)
    dma = pltpu.SemaphoreType.DMA
    slice_shape = (SIZE_Y, 2 * SIZE_Z)
    scratch = [
        pltpu.VMEM((5 * ROWS + 128, ROWS), BF),
        pltpu.VMEM((512, 256), BF),
        pltpu.VMEM((SIZE_Y * 8, ROWS + 16), BF),
        pltpu.VMEM((ROWS, SIZE_Y * 8), BF),
        pltpu.VMEM((32, 8 * 256), BF),
        pltpu.VMEM((CASCADES, 8 * HID, 256), BF),
        pltpu.VMEM((CASCADES, 48, 2 * HID), BF),
        pltpu.VMEM((SIZE_Y, SIZE_Z), jnp.int32),
        pltpu.VMEM((1, 18, HID), BF),
        pltpu.VMEM((1, HID), F32),
        pltpu.VMEM((1, 18, HID), BF),
        pltpu.VMEM((SIZE_X, ROWS, SIZE_Z), BF),
        pltpu.VMEM((16, ROWS, SIZE_Z), F32),
        pltpu.VMEM((16, 32, SIZE_Z), F32),
        pltpu.VMEM((16, *slice_shape), BF),
        pltpu.VMEM((SLOTS, ROWS, SIZE_Z), BF),
        pltpu.VMEM((2, 8, *slice_shape), BF),
        pltpu.VMEM((8, *slice_shape), BF),
        pltpu.VMEM((8, *slice_shape), BF),
        pltpu.VMEM((4, 2, *slice_shape), BF),
        pltpu.VMEM((2, *slice_shape), BF),
        pltpu.VMEM((2, *slice_shape), BF),
        pltpu.VMEM(slice_shape, F32),
        pltpu.VMEM((SLOTS, ROWS, SIZE_Z), BF),
        pltpu.VMEM((SLOTS * SIZE_Y, 2 * SIZE_Z), BF),
        pltpu.VMEM((ROWS, SIZE_Z), BF),
        pltpu.VMEM((CASCADES, 160, 128), BF),
        pltpu.VMEM((CASCADES, 8, 128), F32),
        pltpu.VMEM((ROWS, 2 * SIZE_Z), BF),
        pltpu.VMEM((ROWS, SIZE_Z), BF),
        pltpu.VMEM((SLOTS * SIZE_Y, 2 * SIZE_Z), BF),
        pltpu.VMEM((SLOTS * SIZE_Y, 2 * SIZE_Z), BF),
        pltpu.VMEM((CASCADES, *slice_shape), BF),
        pltpu.VMEM((CASCADES, 3, *slice_shape), BF),
        pltpu.VMEM((SIZE_Y * 8, 3 * SIZE_Z), BF),
        pltpu.VMEM((20, 256, 256), BF),
        pltpu.VMEM((SIZE_Y * 8, 3 * SIZE_Z), BF),
        pltpu.VMEM((CASCADES, SIZE_Y, SIZE_Z), BF),
        dma((11,)),
        dma((SLOTS,)),
        dma((SLOTS,)),
        dma((SLOTS,)),
        dma((3,)),
        dma((2,)),
        dma((6,)),
        dma((8,)),
        dma,
        dma,
        dma((4,)),
        dma((4,)),
        dma((2,)),
        dma((2,)),
        dma((CASCADES, 3)),
        dma((CASCADES, 3)),
        dma((CASCADES,)),
        dma((2,)),
    ]
    result = pl.pallas_call(
        kernel,
        out_shape=pltpu.VMEM((slabs, SIZE_Y, SIZE_Z), BF),
        in_specs=[hbm] * 4 + [smem] + [hbm] * 8,
        out_specs=vmem,
        scratch_shapes=scratch,
        compiler_params=pltpu.CompilerParams(
            collective_id=0, has_side_effects=True, vmem_limit_bytes=62 << 20
        ),
    )(initial, sens, kspace, mask, step_sizes, conv_in, bias_in, conv_out, *tables)
    return result.reshape(1, slabs, 1, SIZE_Y // 2, 2, SIZE_Z)


def solution(mesh):
    return jax.shard_map(
        body,
        mesh=mesh,
        in_specs=(
            P(None, "coil", "cuts", None, None),
            P(None, ("coil", "cuts"), None, None, None, None),
            P(None, ("coil", "cuts"), None, None, None, None),
            P(),
            P("section"),
            P("section", None, None),
            P("section", None),
            P("section", None, None),
        ),
        out_specs=P("section", None, "coil", "cuts", None, None),
        check_vma=False,
    )
```

```python
import functools
import math

import jax
import jax.numpy as jnp
import ml_dtypes
import numpy as np
from jax import lax
from jax.experimental import pallas as pl
from jax.experimental.pallas import tpu as pltpu
from jax.sharding import PartitionSpec as P

MESH = pl.DeviceIdType.MESH
BF = jnp.bfloat16
F32 = jnp.float32
SIZE_X, SIZE_Y, SIZE_Z = 32, 80, 128
ROWS = 2 * SIZE_Y
HID = 128
CASCADES = 4
SLOTS = 16


def dft_table(length, sign):
    ramp = np.arange(length)
    angle = (ramp[:, None] * ramp[None, :] % length) * (2.0 * math.pi / length)
    cosine = np.cos(angle) / math.sqrt(length)
    sine = sign * np.sin(angle) / math.sqrt(length)
    return np.block([[cosine, -sine], [sine, cosine]])


def constants():
    planar = np.arange(ROWS)
    woven = 2 * (planar % SIZE_Y) + planar // SIZE_Y
    deal = np.zeros((ROWS, ROWS))
    deal[planar, woven] = 1.0
    forward_y = dft_table(SIZE_Y, 1.0).T
    back_y = dft_table(SIZE_Y, -1.0).T
    square = np.concatenate([back_y @ deal, forward_y, back_y, deal, deal.T], axis=0)
    wide = np.concatenate([dft_table(SIZE_Z, 1.0), dft_table(SIZE_Z, -1.0)], axis=0)
    taps = np.zeros((SIZE_Y * 8, ROWS + 16))
    gather = np.zeros((ROWS, SIZE_Y * 8))
    for row in range(SIZE_Y):
        taps[row * 8 + 6, ROWS] = 1.0
        for shift in range(3):
            other = row + shift - 1
            if 0 <= other < SIZE_Y:
                for part in range(2):
                    taps[row * 8 + shift * 2 + part, part * SIZE_Y + other] = 1.0
                    gather[part * SIZE_Y + row, other * 8 + shift * 2 + part] = 1.0
    place = np.zeros((32, ROWS))
    for shift_row in range(3):
        for shift_col in range(3):
            for part in range(2):
                place[shift_col * 8 + shift_row * 2 + part, (3 * shift_row + shift_col) * 2 + part] = 1.0
    spread = np.zeros((32, 8 * 256))
    fold = np.zeros((2 * 48, ROWS))
    for shift_col in range(3):
        for r in range(8):
            for i in range(8):
                spread[shift_col * 8 + r, i * 256 + shift_col * 64 + i * 8 + r] = 1.0
            for i in range(2):
                fold[i * 48 + shift_col * 16 + i * 8 + r, shift_col * 8 + r] = 1.0
    square = np.concatenate([square, place, fold], axis=0)
    return [part.astype(ml_dtypes.bfloat16) for part in (square, wide, taps, gather, spread)]


def twiddles():
    first = np.zeros((2, 4, 4), np.complex128)
    second = np.zeros((2, 4, 4, 4), np.complex128)
    for odd in range(2):
        for k in range(4):
            for a in range(4):
                first[odd, k, a] = np.exp(2j * math.pi * k * (2 * a + odd) / 8)
                for b in range(4):
                    position = 8 * b + 2 * a + odd
                    second[odd, k, b, a] = np.exp(2j * math.pi * k * position / SIZE_X) / math.sqrt(SIZE_X)
    return first, second


def dot(a, b):
    return jnp.dot(a, b, preferred_element_type=F32)


def by_lanes(x):
    return jnp.concatenate([x[:SIZE_Y], x[SIZE_Y:]], axis=1)


def by_rows(x):
    return jnp.concatenate([x[:, :SIZE_Z], x[:, SIZE_Z:]], axis=0)


def swap_pair(x):
    a, b, c, d = x[:SIZE_Y, :SIZE_Z], x[SIZE_Y:, :SIZE_Z], x[:SIZE_Y, SIZE_Z:], x[SIZE_Y:, SIZE_Z:]
    return jnp.concatenate(
        [jnp.concatenate([a, b], axis=1), jnp.concatenate([c, d], axis=1)], axis=0
    )


def swap_back(x):
    a, b, c, d = x[:SIZE_Y, :SIZE_Z], x[:SIZE_Y, SIZE_Z:], x[SIZE_Y:, :SIZE_Z], x[SIZE_Y:, SIZE_Z:]
    return jnp.concatenate(
        [jnp.concatenate([a, b], axis=0), jnp.concatenate([c, d], axis=0)], axis=1
    )


def conj_times(s, t):
    s_real, s_imag = s[:, :SIZE_Z].astype(F32), s[:, SIZE_Z:].astype(F32)
    t_real, t_imag = t[:, :SIZE_Z], t[:, SIZE_Z:]
    return s_real * t_real + s_imag * t_imag, s_real * t_imag - s_imag * t_real


def kernel(
    initial, sens, kspace, mask, step, conv_in, bias, conv_out,
    square_in, wide_in, taps_in, gather_in, spread_in,
    out,
    square, wide, taps_sel, gather_sel, spread, first_block, second_block, mask_here, conv_in_here, bias_here, conv_out_here,
    kbuf, ubuf, gbuf, tbuf, sown, bpart, brecv, bsum, yrecv, zsum, bin_, btot,
    srecv, splan, ibuf, wbuf, fbuf, mplan, mwoven,
    vbuf, wspec, partial, arrived, tapbuf, hidbuf, prodbuf, obuf,
    local_sem, own_sem, s_send, s_recv, i_send, i_recv, w_send, w_recv,
    x_send, x_recv, y_send, y_recv, b_send, b_recv, r_send, r_recv, o_send, o_recv,
):
    sec, pos, core = lax.axis_index("section"), lax.axis_index("coil"), lax.axis_index("cuts")
    row, col = pos // 8, pos % 8
    odd_col = col % 2
    sign = 1 - 2 * ((col + row) % 2)
    odd = sec % 2
    slab = sec // 2
    home = odd_col == odd

    def at(section, y, z, c):
        return (section, y * 8 + z, c)

    twin = (col + sign + 8) % 8
    mates = [at(sec, row, col, 1 - core), at(sec, row, twin, core), at(sec, row, twin, 1 - core)]
    others = [((sec + k) % 4, pos, core) for k in (1, 2, 3)]

    def toward(j, dy):
        z = (col + (1 - 2 * (j % 2)) * (1 - 2 * (dy % 2)) * sign * j + 8) % 8
        y = (row + dy) % 4
        pair = (z + 1 - 2 * ((z + y) % 2) + 8) % 8
        held = jnp.where(z % 2 == odd, z, pair)
        return at(sec, y, z, core), 8 * y + held, y * 4 + held // 2

    barrier = pltpu.get_barrier_semaphore()
    greet = [at(sec, (row + dy) % 4, (col - sign * j + 8) % 8, core) for j in (3, 2, 1, 0) for dy in (2, 1, 3, 0)][:-1]
    for device in greet + others + mates:
        pl.semaphore_signal(barrier, inc=1, device_id=device, device_id_type=MESH)

    loads = [
        pltpu.make_async_copy(square_in, square, local_sem.at[0]),
        pltpu.make_async_copy(kspace.at[slab], kbuf, local_sem.at[1]),
        pltpu.make_async_copy(wide_in, wide, local_sem.at[2]),
        pltpu.make_async_copy(taps_in, taps_sel, local_sem.at[3]),
        pltpu.make_async_copy(gather_in, gather_sel, local_sem.at[4]),
        pltpu.make_async_copy(mask.at[slab], mask_here, local_sem.at[5]),
        pltpu.make_async_copy(conv_in, conv_in_here, local_sem.at[6]),
        pltpu.make_async_copy(bias, bias_here, local_sem.at[7]),
        pltpu.make_async_copy(conv_out, conv_out_here, local_sem.at[8]),
        pltpu.make_async_copy(spread_in, spread, local_sem.at[10]),
    ]
    half = pl.multiple_of(core * SIZE_Y, SIZE_Y)
    own_half = pltpu.make_async_copy(initial.at[slab], ibuf.at[pl.ds(half, SIZE_Y)], local_sem.at[9])
    own_loads = []
    for slot in range(SLOTS):
        _, position, _ = toward(slot // 4, slot % 4)
        own_loads.append(pltpu.make_async_copy(sens.at[slab, position], sown.at[slot], own_sem.at[slot]))
    for load in loads + own_loads:
        load.start()

    def remote(src, dst, send, recv, device):
        return pltpu.make_async_remote_copy(
            src_ref=src, dst_ref=dst, send_sem=send, recv_sem=recv, device_id=device, device_id_type=MESH
        )

    for load in (loads[0], loads[5]):
        load.wait()
    plane = mask_here[...].astype(F32).astype(BF)
    both = jnp.concatenate([plane, plane], axis=0)
    mplan[...] = jnp.concatenate([both, both], axis=1)
    mwoven[...] = dot(square[4 * ROWS : 5 * ROWS], both).astype(BF)
    loads[1].wait()

    fold = (1 - 2 * odd).astype(F32)

    def data_rows(n, _):
        masked = mwoven[...]
        two = jnp.concatenate([kbuf[n] * masked, kbuf[n + 16] * masked], axis=1)
        done = dot(square[0:ROWS], two)
        ubuf[n] = done[:, :SIZE_Z] + fold * done[:, SIZE_Z:]
        return 0

    lax.fori_loop(0, 16, data_rows, 0, unroll=4)

    arrived[CASCADES - 1] = jnp.zeros((3, SIZE_Y, 2 * SIZE_Z), BF)
    pl.semaphore_wait(barrier, len(greet) + 6)

    image_copies = [
        remote(initial.at[slab], ibuf.at[pl.ds(half, SIZE_Y)], i_send.at[k], i_recv.at[core], mates[k])
        for k in range(3)
    ]

    @pl.when(home)
    def _():
        for copy in image_copies:
            copy.start()
        own_half.start()

    sens_copies = []
    for slot in range(1, SLOTS):
        device, position, _ = toward(slot // 4, slot % 4)
        sens_copies.append(
            remote(sens.at[slab, position], srecv.at[slot], s_send.at[slot], s_recv.at[slot], device)
        )
    for copy in sens_copies:
        copy.start()

    first, second = twiddles()

    def coefficient(table):
        even_value, odd_value = complex(table[0]), complex(table[1])
        return (
            jnp.where(odd == 0, np.float32(even_value.real), np.float32(odd_value.real)),
            jnp.where(odd == 0, np.float32(even_value.imag), np.float32(odd_value.imag)),
        )

    def weighted(terms):
        real, imag = None, None
        for (w_real, w_imag), (v_real, v_imag) in terms:
            r = w_real * v_real - w_imag * v_imag
            i = w_real * v_imag + w_imag * v_real
            real, imag = (r, i) if real is None else (real + r, imag + i)
        return real, imag

    def x_pass(chunk, _):
        top = pl.multiple_of(chunk * 16, 16)
        below = pl.multiple_of(SIZE_Y + chunk * 16, 16)
        for n in range(4):
            u = [(ubuf[n + 4 * k, pl.ds(top, 16)], ubuf[n + 4 * k, pl.ds(below, 16)]) for k in range(4)]
            for a in range(4):
                real, imag = weighted([(coefficient(first[:, k, a]), u[k]) for k in range(4)])
                gbuf[n * 4 + a, 0:16] = real
                gbuf[n * 4 + a, 16:32] = imag
        for a in range(4):
            g = [(gbuf[n * 4 + a, 0:16], gbuf[n * 4 + a, 16:32]) for n in range(4)]
            for b in range(4):
                real, imag = weighted([(coefficient(second[:, n, b, a]), g[n]) for n in range(4)])
                tbuf[b * 4 + a, pl.ds(top, 16), 0:SIZE_Z] = real.astype(BF)
                tbuf[b * 4 + a, pl.ds(top, 16), SIZE_Z:] = imag.astype(BF)
        return 0

    lax.fori_loop(0, 5, x_pass, 0)
    loads[2].wait()
    for load in own_loads:
        load.wait()

    def share(parity):
        def one(q, _):
            jh = q // 2
            j = 2 * jh + parity
            dy = 2 * (q % 2)
            _, _, e0 = toward(j, dy)
            _, _, e1 = toward(j, dy + 1)
            done = dot(jnp.concatenate([tbuf[e0], tbuf[e1]], axis=0), wide[256:512])
            slot = j * 4 + dy
            pair = dot(square[3 * ROWS : 4 * ROWS], jnp.concatenate([sown[slot], sown[slot + 1]], axis=1))
            pair = swap_pair(pair)
            for k in range(2):
                real, imag = conj_times(pair[k * SIZE_Y : (k + 1) * SIZE_Y], done[k * SIZE_Y : (k + 1) * SIZE_Y])
                bpart[parity, (dy + k) * 2 + jh] = jnp.concatenate([real, imag], axis=1).astype(BF)
            return 0

        lax.fori_loop(0, 4, one, 0, unroll=4)

    share(1 - core)
    exchange = remote(bpart.at[1 - core], brecv, x_send, x_recv, mates[0])
    exchange.start()
    share(core)
    exchange.wait_recv()

    for q in range(8):
        bsum[q] = (bpart[core, q].astype(F32) + brecv[q].astype(F32)).astype(BF)
    row_copies = [
        remote(bsum.at[pl.ds(2 * dy, 2)], yrecv.at[dy], y_send.at[dy], y_recv.at[dy], at(sec, (row + dy) % 4, col, core))
        for dy in (1, 2, 3)
    ]
    for copy in row_copies:
        copy.start()

    for load in (loads[6], loads[7], loads[8]):
        load.wait()
    bias_rows = jnp.broadcast_to(bias_here[...], (32, 128))
    high = bias_rows.astype(BF).astype(F32)
    middle = (bias_rows - high).astype(BF).astype(F32)
    low = bias_rows - high - middle
    which = lax.broadcasted_iota(jnp.int32, (32, 128), 0)
    stacked = jnp.where(which == 6, high, jnp.where(which == 14, middle, jnp.where(which == 22, low, 0.0)))
    place = square[5 * ROWS : 5 * ROWS + 32][:, 0:18]
    first_layer = dot(place, conv_in_here[0]) + stacked
    first_layer = jnp.concatenate([0.5 * first_layer, jnp.zeros((96, 128), F32)], axis=0)
    wbuf[sec, 0:128] = first_layer.T.astype(BF)
    wbuf[sec, 128:160] = dot(place, conv_out_here[0]).astype(BF)
    fbuf[sec] = jnp.full((8, 128), step[0], F32)
    net_copies = []
    for k in range(3):
        net_copies.append(remote(wbuf.at[sec], wbuf.at[sec], w_send.at[k], w_recv.at[sec], others[k]))
        net_copies.append(remote(fbuf.at[sec], fbuf.at[sec], w_send.at[3 + k], w_recv.at[4 + sec], others[k]))
    for copy in net_copies:
        copy.start()

    def arrival(index):
        return remote(ibuf.at[pl.ds(index * SIZE_Y, SIZE_Y)], ibuf.at[pl.ds(index * SIZE_Y, SIZE_Y)],
                      i_send.at[0], i_recv.at[index], mates[0])

    @pl.when(jnp.logical_or(jnp.logical_not(home), core == 1))
    def _():
        arrival(0).wait_recv()

    @pl.when(jnp.logical_or(jnp.logical_not(home), core == 0))
    def _():
        arrival(1).wait_recv()

    @pl.when(home)
    def _():
        own_half.wait()

    image = by_lanes(dot(square[3 * ROWS : 4 * ROWS], ibuf[...]))

    def net_arrival(c, buf, index):
        return remote(buf.at[c], buf.at[c], w_send.at[0], w_recv.at[index], others[0])

    for k in range(3):
        other = (sec + k + 1) % 4
        net_arrival(other, wbuf, other).wait_recv()
        net_arrival(other, fbuf, 4 + other).wait_recv()

    loads[9].wait()

    def blocks(c, _):
        layer = wbuf[c, 0:128][:, 0:32]
        for i in range(8):
            first_block[c, i * 128 : (i + 1) * 128] = dot(layer, spread[:, i * 256 : (i + 1) * 256]).astype(BF)
        for i in range(2):
            rows = square[5 * ROWS + 32 + 48 * i : 5 * ROWS + 80 + 48 * i][:, 0:32]
            second_block[c, :, i * 128 : (i + 1) * 128] = dot(rows, wbuf[c, 128:160]).astype(BF)
        return 0

    lax.fori_loop(0, CASCADES, blocks, 0)

    for copy in row_copies:
        copy.wait_recv()
    for jh in range(2):
        total = bsum[jh].astype(F32)
        for dy in range(1, 4):
            total = total + yrecv[dy, jh].astype(F32)
        zsum[jh] = total.astype(BF)
    data_copies = [
        remote(zsum.at[jh], bin_.at[jh], b_send.at[jh], b_recv.at[jh], toward(2 * jh + core, 0)[0]) for jh in range(2)
    ]
    data_copies[1].start()

    @pl.when(core == 0)
    def _():
        bin_[0] = zsum[0]

    @pl.when(core == 1)
    def _():
        data_copies[0].start()

    for k in range(8):
        if k:
            sens_copies[2 * k - 1].wait_recv()
        sens_copies[2 * k].wait_recv()
        left = sown[0] if k == 0 else srecv[2 * k]
        pair = dot(square[3 * ROWS : 4 * ROWS], jnp.concatenate([left, srecv[2 * k + 1]], axis=1))
        splan[pl.ds(k * ROWS, ROWS)] = swap_pair(pair).astype(BF)

    loads[3].wait()
    loads[4].wait()
    lane = lax.broadcasted_iota(jnp.int32, (ROWS, SIZE_Z), 1)

    def moved_right(x):
        return jnp.where(lane == 0, 0.0, pltpu.roll(x, 1, 1))

    def moved_left(x):
        return jnp.where(lane == SIZE_Z - 1, 0.0, pltpu.roll(x, SIZE_Z - 1, 1))

    def operator(image):
        real, imag = image[:, :SIZE_Z], image[:, SIZE_Z:]
        for k in range(SLOTS):
            s = splan[pl.ds(k * SIZE_Y, SIZE_Y)].astype(F32)
            s_real, s_imag = s[:, :SIZE_Z], s[:, SIZE_Z:]
            v = jnp.concatenate([s_real * real - s_imag * imag, s_real * imag + s_imag * real], axis=1)
            vbuf[pl.ds(k * SIZE_Y, SIZE_Y)] = v.astype(BF)
        for k in range(8):
            spectrum = dot(vbuf[pl.ds(k * ROWS, ROWS)], wide[0:256]).astype(BF)
            wspec[pl.ds(k * ROWS, ROWS)] = swap_back(spectrum)
        for k in range(8):
            predicted = dot(square[ROWS : 2 * ROWS], wspec[pl.ds(k * ROWS, ROWS)]).astype(BF)
            vbuf[pl.ds(k * ROWS, ROWS)] = predicted * mplan[...]
        for k in range(8):
            back = dot(square[2 * ROWS : 3 * ROWS], vbuf[pl.ds(k * ROWS, ROWS)]).astype(BF)
            wspec[pl.ds(k * ROWS, ROWS)] = swap_pair(back)
        total_real, total_imag = jnp.zeros((SIZE_Y, SIZE_Z), F32), jnp.zeros((SIZE_Y, SIZE_Z), F32)
        for k in range(8):
            back = dot(wspec[pl.ds(k * ROWS, ROWS)], wide[256:512])
            for i in range(2):
                s = splan[pl.ds(k * ROWS + i * SIZE_Y, SIZE_Y)]
                r, m = conj_times(s, back[i * SIZE_Y : (i + 1) * SIZE_Y])
                total_real, total_imag = total_real + r, total_imag + m
        return jnp.concatenate([total_real, total_imag], axis=1)

    def refine(image, c):
        planar = by_rows(image)
        three = jnp.concatenate([moved_right(planar), planar, moved_left(planar)], axis=1)
        lift = jnp.where(lax.broadcasted_iota(jnp.int32, (16, 3 * SIZE_Z), 0) == 0, 1.0, 0.0)
        operand = jnp.concatenate([three, lift], axis=0).astype(BF)
        tapbuf[...] = dot(taps_sel[...], operand).astype(BF)
        for g in range(5):
            near = [
                jnp.concatenate(
                    [tapbuf[128 * g + 64 * k : 128 * g + 64 * (k + 1), d * 128 : (d + 1) * 128] for d in range(3)], axis=0
                )
                for k in range(2)
            ]
            near = jnp.concatenate(near, axis=1)
            for t in range(4):
                pre = dot(first_block[c, t * 256 : (t + 1) * 256][:, 0:192], near).astype(BF)
                hidbuf[g * 4 + t] = pre + pre * jnp.tanh(pre)
        for g in range(5):
            for t in range(4):
                product = dot(second_block[c], hidbuf[g * 4 + t]).astype(BF)
                for k in range(2):
                    top = 128 * g + 64 * k + 16 * t
                    for d in range(3):
                        prodbuf[top : top + 16, d * 128 : (d + 1) * 128] = product[
                            d * 16 : (d + 1) * 16, k * 128 : (k + 1) * 128
                        ]
        summed = dot(gather_sel[...], prodbuf[...])
        total = moved_right(summed[:, 0:128]) + summed[:, 128:256] + moved_left(summed[:, 256:384])
        return by_lanes(total)

    def data_arrival(q):
        return remote(zsum.at[q], bin_.at[q], b_send.at[q], b_recv.at[q], mates[0])

    def out_copy(c):
        return remote(obuf.at[c], out.at[slab], o_send.at[c], o_recv.at[slab], (c, pos, core))

    def last_copy(k, for_core):
        c, rows = CASCADES - 1, pl.ds(pl.multiple_of(32 * for_core, 16), 48)
        return remote(
            partial.at[c, rows], arrived.at[c, k, rows], r_send.at[c, k], r_recv.at[c, k], mates[k]
        )

    last_sends = [last_copy(0, 1 - core), last_copy(1, core), last_copy(2, 1 - core)]

    def cascade(c, image):
        sent = operator(image)

        @pl.when(c == 0)
        def _():
            @pl.when(core == 1)
            def _():
                data_arrival(0).wait_recv()

            data_arrival(1).wait_recv()
            btot[...] = bin_[0].astype(F32) + bin_[1].astype(F32)

        partial[c] = (sent - btot[...]).astype(BF)
        copies = [
            remote(partial.at[c], arrived.at[c, k], r_send.at[c, k], r_recv.at[c, k], mates[k]) for k in range(3)
        ]
        @pl.when(c < CASCADES - 1)
        def _():
            for copy in copies[::-1]:
                copy.start()

        @pl.when(c == CASCADES - 1)
        def _():
            for copy in last_sends[::-1]:
                copy.start()

        refined = refine(image, c)

        @pl.when(c < CASCADES - 1)
        def _():
            for copy in copies:
                copy.wait_recv()

        @pl.when(c == CASCADES - 1)
        def _():
            for k in range(3):
                last_copy(k, core).wait_recv()

        total = partial[c].astype(F32)
        for k in range(3):
            total = total + arrived[c, k].astype(F32)
        updated = (image + fbuf[c, 0:1, 0:1] * total + refined).astype(BF)

        @pl.when(home)
        def _():
            base = pl.multiple_of(4 * ROWS + core * SIZE_Y, 16)
            obuf[c] = dot(square[pl.ds(base, SIZE_Y)], by_rows(updated)).astype(BF)

            @pl.when(c == sec)
            def _():
                out[slab] = obuf[c]

            @pl.when(c != sec)
            def _():
                out_copy(c).start()

        return updated.astype(F32)

    lax.fori_loop(0, CASCADES, cascade, image)

    for c in range(CASCADES):
        for k in range(3):
            if c < CASCADES - 1:
                remote(partial.at[c], arrived.at[c, k], r_send.at[c, k], r_recv.at[c, k], mates[k]).wait_send()
            else:
                last_sends[k].wait_send()

        @pl.when(jnp.logical_and(home, c != sec))
        def _():
            out_copy(c).wait_send()

    for m in range(2):

        @pl.when(2 * m + odd_col != sec)
        def _():
            remote(obuf.at[0], out.at[m], o_send.at[0], o_recv.at[m], others[0]).wait_recv()

    @pl.when(home)
    def _():
        for copy in image_copies:
            copy.wait_send()

    for copy in sens_copies + net_copies + [exchange, data_copies[1]] + row_copies:
        copy.wait_send()

    @pl.when(core == 1)
    def _():
        data_copies[0].wait_send()


def body(initial, sens, kspace, mask, step_sizes, conv_in, bias_in, conv_out):
    slabs = initial.shape[0]
    initial = initial.reshape(slabs, SIZE_Y, SIZE_Z)
    sens = sens.reshape(slabs, SIZE_X, ROWS, SIZE_Z)
    kspace = kspace.reshape(slabs, SIZE_X, ROWS, SIZE_Z)
    conv_in = jnp.swapaxes(conv_in, 1, 2)
    tables = [jnp.asarray(part) for part in constants()]
    vmem = pl.BlockSpec(memory_space=pltpu.VMEM)
    hbm = pl.BlockSpec(memory_space=pltpu.HBM)
    smem = pl.BlockSpec(memory_space=pltpu.SMEM)
    dma = pltpu.SemaphoreType.DMA
    slice_shape = (SIZE_Y, 2 * SIZE_Z)
    scratch = [
        pltpu.VMEM((5 * ROWS + 128, ROWS), BF),
        pltpu.VMEM((512, 256), BF),
        pltpu.VMEM((SIZE_Y * 8, ROWS + 16), BF),
        pltpu.VMEM((ROWS, SIZE_Y * 8), BF),
        pltpu.VMEM((32, 8 * 256), BF),
        pltpu.VMEM((CASCADES, 8 * HID, 256), BF),
        pltpu.VMEM((CASCADES, 48, 2 * HID), BF),
        pltpu.VMEM((SIZE_Y, SIZE_Z), jnp.int32),
        pltpu.VMEM((1, 18, HID), BF),
        pltpu.VMEM((1, HID), F32),
        pltpu.VMEM((1, 18, HID), BF),
        pltpu.VMEM((SIZE_X, ROWS, SIZE_Z), BF),
        pltpu.VMEM((16, ROWS, SIZE_Z), F32),
        pltpu.VMEM((16, 32, SIZE_Z), F32),
        pltpu.VMEM((16, *slice_shape), BF),
        pltpu.VMEM((SLOTS, ROWS, SIZE_Z), BF),
        pltpu.VMEM((2, 8, *slice_shape), BF),
        pltpu.VMEM((8, *slice_shape), BF),
        pltpu.VMEM((8, *slice_shape), BF),
        pltpu.VMEM((4, 2, *slice_shape), BF),
        pltpu.VMEM((2, *slice_shape), BF),
        pltpu.VMEM((2, *slice_shape), BF),
        pltpu.VMEM(slice_shape, F32),
        pltpu.VMEM((SLOTS, ROWS, SIZE_Z), BF),
        pltpu.VMEM((SLOTS * SIZE_Y, 2 * SIZE_Z), BF),
        pltpu.VMEM((ROWS, SIZE_Z), BF),
        pltpu.VMEM((CASCADES, 160, 128), BF),
        pltpu.VMEM((CASCADES, 8, 128), F32),
        pltpu.VMEM((ROWS, 2 * SIZE_Z), BF),
        pltpu.VMEM((ROWS, SIZE_Z), BF),
        pltpu.VMEM((SLOTS * SIZE_Y, 2 * SIZE_Z), BF),
        pltpu.VMEM((SLOTS * SIZE_Y, 2 * SIZE_Z), BF),
        pltpu.VMEM((CASCADES, *slice_shape), BF),
        pltpu.VMEM((CASCADES, 3, *slice_shape), BF),
        pltpu.VMEM((SIZE_Y * 8, 3 * SIZE_Z), BF),
        pltpu.VMEM((20, 256, 256), BF),
        pltpu.VMEM((SIZE_Y * 8, 3 * SIZE_Z), BF),
        pltpu.VMEM((CASCADES, SIZE_Y, SIZE_Z), BF),
        dma((11,)),
        dma((SLOTS,)),
        dma((SLOTS,)),
        dma((SLOTS,)),
        dma((3,)),
        dma((2,)),
        dma((6,)),
        dma((8,)),
        dma,
        dma,
        dma((4,)),
        dma((4,)),
        dma((2,)),
        dma((2,)),
        dma((CASCADES, 3)),
        dma((CASCADES, 3)),
        dma((CASCADES,)),
        dma((2,)),
    ]
    result = pl.pallas_call(
        kernel,
        out_shape=pltpu.VMEM((slabs, SIZE_Y, SIZE_Z), BF),
        in_specs=[hbm] * 4 + [smem] + [hbm] * 8,
        out_specs=vmem,
        scratch_shapes=scratch,
        compiler_params=pltpu.CompilerParams(
            collective_id=0, has_side_effects=True, vmem_limit_bytes=62 << 20
        ),
    )(initial, sens, kspace, mask, step_sizes, conv_in, bias_in, conv_out, *tables)
    return result.reshape(1, slabs, 1, SIZE_Y // 2, 2, SIZE_Z)


def solution(mesh):
    return jax.shard_map(
        body,
        mesh=mesh,
        in_specs=(
            P(None, "coil", "cuts", None, None),
            P(None, ("coil", "cuts"), None, None, None, None),
            P(None, ("coil", "cuts"), None, None, None, None),
            P(),
            P("section"),
            P("section", None, None),
            P("section", None),
            P("section", None, None),
        ),
        out_specs=P("section", None, "coil", "cuts", None, None),
        check_vma=False,
    )
```
